32 devices in a mesh: region: 4 (over z), dom: 4 (over y, core), segment: 2 (over x).
Axes of the slice: x: 2, y: 2, z: 4, core: 2. Of those that a mesh axis runs over, the one named last changes fastest.
Arguments:
- stored: float32 [4, 2, 5, 125, 4096], P('segment', None, None, None, ('region', 'dom')), may hold values from -6 to 6
- new_owner: int32 [4096, 1], P(('region', 'dom')), may hold values from 0 to 3; in each aligned block of 256 rows (0 to 255, 256 to 511, ...) at most 96 rows name the same one
- adjoint: float32 [5, 125, 6144], P(None, None, ('region', 'dom')), may hold values from -6 to 6
- deriv: float32 [3, 125, 125], replicated, may hold values from -0.5 to 0.5
- mixing: float32 [3, 5, 5], replicated, may hold values from -2.5 to 2.5
- face_lists: int32 [2, 2048], P(None, ('region', 'dom')), may hold values from 0 to 383
- param_map: int32 [6144], P(('region', 'dom')), may hold values from 0 to 4095
Outputs:
- adjoint_out: float32 [5, 125, 6144], P(None, None, ('region', 'dom'))
- gradient: float32 [4096], replicated
The draws below stay inside these ranges and needn't reach their ends.
Inputs may be any that keep to these rules, and one draw needn't show every extreme that they name: `new_owner`: within the 256 elements of one old partition no new partition is named more than 96 times, a bound that some block reaches. `face_lists`: slot numbers within a current partition, repeats allowed.
All inputs are finite; a program needn't handle non-finite values.
Results may differ from the reference program's by a relative error of at most 0.0001.
Values sent between devices are 32-bit elements; how exact they have to be, the bound alone decides.
No kernel may reach another device: no remote copies, remote signals or barrier semaphores. Data moves between devices by JAX's collectives and lax.ppermute only.
A program may use at most 64 MiB of HBM per device.

```python
import math
import jax
import jax.numpy as jnp
import numpy as np
from jax import lax

FIELDS = 5
NODES = 125
FACE_NODES = 25
RK_SEGMENTS = 4
STEPS = 2
PARAMS = 4096
ELEM_DEV = 256
FACES = 128
SLOTS = 384
CAP = 96
ELEMS_OLD = 4096
ELEMS_CUR = 6144
N_REGION = 4
N_DOM = 4


def plant(values, key, low, high):
    shape = values.shape
    index_at = [jax.random.randint(jax.random.fold_in(key, axis), (), 0, shape[axis]) for axis in range(len(shape))]
    values = values.at[tuple(index_at)].set(low)
    longest = shape.index(max(shape))
    index_at[longest] = (index_at[longest] + 1) % shape[longest]
    return values.at[tuple(index_at)].set(high)


def levels(own_key, shape, pieces, least, high):
    loudness, own = 1.0, jax.random.fold_in(own_key, 6)
    for dim, blocks in pieces:
        steps = jnp.exp(jax.random.uniform(jax.random.fold_in(own, dim), (blocks,), jnp.float32, least / len(pieces), high / len(pieces)))
        loudness = loudness * jnp.repeat(steps, shape[dim] // blocks).reshape([-1 if axis == dim else 1 for axis in range(len(shape))])
    return loudness


def routed_block(stream_key, own, number, rows, amount, top, bound, lean):
    order = jax.random.permutation(stream_key, amount)
    heavy_load, ordinary = load_shares(amount, rows * top, bound, lean, True), load_shares(amount, rows * top, bound, lean, False)
    places = jnp.arange(amount)

    def named(lengths, rotation):
        used = int((lengths > 0).sum())
        fixed = max(1, used // 4)
        passed = fixed + (places - fixed + rotation * (used - fixed)) % max(1, amount - fixed)
        return jnp.zeros((amount,), jnp.int32).at[order[jnp.where(places < fixed, places, passed)]].set(jnp.asarray(lengths, jnp.int32))

    lengths = jnp.where(number % 4 == 0, named(heavy_load, number // 4), named(ordinary, number - number // 4 - 1))
    mixed = jax.random.permutation(jax.random.fold_in(own, 3), amount)
    giver, sink = mixed[0:amount // 2 * 2:2], mixed[1:amount // 2 * 2:2]
    slack = jnp.minimum(lengths[giver] - 1, bound - lengths[sink]) // 2
    slack = jnp.where((giver == order[0]) | (sink == order[0]) | (lengths[sink] == 0), 0, jnp.maximum(slack, 0))
    passed = jax.random.randint(jax.random.fold_in(own, 4), (amount // 2,), 0, 1 << 20) % (slack + 1)
    lengths = lengths.at[giver].add(-passed).at[sink].add(passed)
    items = jnp.searchsorted(jnp.cumsum(lengths), jnp.arange(rows * top), side="right").astype(jnp.int32)
    listing = items.reshape(top, rows).T
    listing = listing[jax.random.permutation(jax.random.fold_in(own, 1), rows)]
    rotation = jax.random.randint(jax.random.fold_in(own, 2), (rows, 1), 0, top)
    return jnp.take_along_axis(listing, (jnp.arange(top)[None, :] + rotation) % top, axis=1)


def load_shares(count, total, reach, skew, full):
    weights = [(1 << 20) // math.isqrt(standing ** skew) + 1 for standing in range(1, count + 1)]
    largest = reach if full else min(reach, max(-(-total // count), total * weights[0] // sum(weights)))
    least = 1 if total - largest >= count - 1 else 0
    counts, rest = [largest] + [least] * (count - 1), total - largest - least * (count - 1)
    while rest > 0:
        movable = [i for i in range(1, count) if counts[i] < largest] or [i for i in range(1, count) if counts[i] < reach]
        mass, remaining = sum([weights[i] for i in movable]), rest
        for i in movable:
            addition = min(reach - counts[i], max(1, remaining * weights[i] // mass), rest)
            counts[i] = counts[i] + addition
            rest = rest - addition
    return np.array(counts)


def gaussian(stream_key, shape, width, most, split=(), held_as=jnp.bfloat16):
    values = jax.random.normal(stream_key, shape, jnp.float32) * width
    if len(split) > 0:
        values = levels(stream_key, shape, split, -0.22, 0.18) * values
    return jnp.clip(values, min=-most, max=most).astype(held_as)


def setup_inputs(seed: int = 0) -> dict:
    key_of = jax.random.split(jax.random.key(seed), 8)
    stored = gaussian(key_of[0], (RK_SEGMENTS, STEPS, FIELDS, NODES, ELEMS_OLD), 1.0, 6.0, ((0, 2), (4, 16)), jnp.float32)
    new_owner_keys = jax.random.split(jax.random.fold_in(key_of[1], 1), ELEMS_OLD // ELEM_DEV)
    new_owner_turns = jax.random.permutation(jax.random.fold_in(key_of[1], 3), ELEMS_OLD // ELEM_DEV)
    new_owner = jax.vmap(lambda own, number: routed_block(jax.random.fold_in(key_of[1], 2), own, number, ELEM_DEV, N_DOM, 1, CAP, 2))(new_owner_keys, new_owner_turns).reshape((ELEMS_OLD, 1))
    adjoint = gaussian(key_of[2], (FIELDS, NODES, ELEMS_CUR), 1.0, 6.0, ((2, 16),), jnp.float32)
    deriv = gaussian(key_of[3], (3, NODES, NODES), NODES ** -0.5, 0.5, (), jnp.float32)
    mixing = gaussian(key_of[4], (3, FIELDS, FIELDS), FIELDS ** -0.5, 2.5, (), jnp.float32)
    face_lists = plant(jax.random.randint(key_of[5], (2, N_REGION * N_DOM * FACES), 0, SLOTS), jax.random.fold_in(key_of[5], 1), 0, SLOTS - 1).astype(jnp.int32)
    param_map = plant(jax.random.randint(key_of[6], (ELEMS_CUR,), 0, PARAMS), jax.random.fold_in(key_of[6], 1), 0, PARAMS - 1).astype(jnp.int32)
    return {"stored": stored, "new_owner": new_owner, "adjoint": adjoint, "deriv": deriv, "mixing": mixing, "face_lists": face_lists, "param_map": param_map}


rk_weights = (1.0 / 6.0, 1.0 / 3.0, 1.0 / 3.0, 1.0 / 6.0)
step_size = 0.5
face_gain = 0.5


def volume_term(state, adjoint_now, deriv, mixing):
    squashed = jnp.tanh(state)
    projected = jnp.sum(squashed * adjoint_now, axis=0)
    flux_part = squashed * projected[None]
    result = jnp.zeros_like(adjoint_now)
    for direction_pos in range(3):
        weighted = jnp.einsum("gf,gme->fme", mixing[direction_pos], adjoint_now, precision=lax.Precision.HIGHEST) + flux_part
        result = result + jnp.einsum("mn,fme->fne", deriv[direction_pos], weighted, precision=lax.Precision.HIGHEST)
    return result


def migrate_index(new_owner):
    target = new_owner[:, 0].astype(jnp.int32).reshape(N_REGION, N_DOM, ELEM_DEV)
    one_hot = (target[..., None] == jnp.arange(N_DOM, dtype=jnp.int32)).astype(jnp.int32)
    earlier = jnp.cumsum(one_hot, axis=2) - one_hot
    position = jnp.sum(earlier * one_hot, axis=-1).astype(jnp.int32)
    region_ids = jnp.arange(N_REGION, dtype=jnp.int32)[:, None, None]
    source_ids = jnp.arange(N_DOM, dtype=jnp.int32)[None, :, None]
    index = (region_ids * N_DOM + target) * SLOTS + source_ids * CAP + position
    return index.reshape(-1).astype(jnp.int32)


def face_term(adjoint_now, face_lists):
    grid = adjoint_now.reshape(FIELDS, NODES, N_REGION, N_DOM, SLOTS).transpose(2, 3, 0, 1, 4)
    lists = face_lists.astype(jnp.int32).reshape(2, N_REGION, N_DOM, FACES)

    def pick(block, low_list, high_list):
        return (jnp.take(block[:, :FACE_NODES], low_list, axis=2),
                jnp.take(block[:, NODES - FACE_NODES:], high_list, axis=2))

    own_low, own_high = jax.vmap(jax.vmap(pick))(grid, lists[0], lists[1])
    blank = jnp.zeros_like(own_low[:1])
    near_low = jnp.concatenate([blank, own_high[:-1]], axis=0)
    near_high = jnp.concatenate([own_low[1:], blank], axis=0)

    def place(low_list, high_list, jump_low, jump_high):
        added = jnp.zeros((FIELDS, NODES, SLOTS), jnp.float32)
        added = added.at[:, :FACE_NODES, low_list].add(face_gain * jump_low)
        added = added.at[:, NODES - FACE_NODES:, high_list].add(face_gain * jump_high)
        return added

    added = jax.vmap(jax.vmap(place))(lists[0], lists[1], near_low - own_low, near_high - own_high)
    return added.transpose(2, 3, 0, 1, 4).reshape(FIELDS, NODES, ELEMS_CUR)


def reference(stored, new_owner, adjoint, deriv, mixing, face_lists, param_map):
    index = migrate_index(new_owner)
    adjoint_now = adjoint
    gradient = jnp.zeros((PARAMS,), jnp.float32)
    for which_step in range(STEPS):
        total = jnp.zeros_like(adjoint)
        for segment_pos in range(RK_SEGMENTS):
            state = jnp.zeros((FIELDS, NODES, ELEMS_CUR), jnp.float32).at[..., index].set(stored[segment_pos, which_step])
            term = volume_term(state, adjoint_now, deriv, mixing)
            total = total + rk_weights[segment_pos] * term
            density = jnp.mean(term * state, axis=(0, 1))
            gradient = gradient.at[param_map.astype(jnp.int32)].add(rk_weights[segment_pos] * density)
        adjoint_now = adjoint_now + step_size * (total + face_term(adjoint_now, face_lists))
    return adjoint_now, gradient
```

```python
import functools

import jax
import jax.numpy as jnp
from jax import lax
from jax.experimental import pallas as pl
from jax.experimental.pallas import tpu as pltpu
from jax.sharding import PartitionSpec as P

FACE_NODES = 25
STEPS = 2
PARAMS = 4096
LANES = 128

rk_weights = (1.0 / 6.0, 1.0 / 3.0, 1.0 / 3.0, 1.0 / 6.0)
step_size = 0.5
face_gain = 0.5

F32 = jnp.float32
BF16 = jnp.bfloat16
VMEM = pl.BlockSpec(memory_space=pltpu.VMEM)
SMEM = pl.BlockSpec(memory_space=pltpu.SMEM)
NN = (((1,), (0,)), ((), ()))
NT = (((1,), (1,)), ((), ()))


def call(body, outs, specs, scratch=(), flops=1e8, moved=2e6):
    return pl.pallas_call(
        body,
        out_shape=outs,
        in_specs=specs,
        out_specs=jax.tree.map(lambda _: VMEM, outs),
        scratch_shapes=list(scratch),
        compiler_params=pltpu.CompilerParams(vmem_limit_bytes=40 * 2**20),
        cost_estimate=pl.CostEstimate(
            flops=int(flops), bytes_accessed=int(moved), transcendentals=0
        ),
    )


def shape(*dims, dtype=F32):
    return jax.ShapeDtypeStruct(dims, dtype)


def halves(value):
    top = value.astype(BF16)
    return top, (value - top.astype(F32)).astype(BF16)


def dot(a, b, dims=NN):
    return lax.dot_general(a, b, dims, preferred_element_type=F32)


def pick(value, chosen, dims=NN):
    top, rest = halves(value)
    return dot(top, chosen, dims) + dot(rest, chosen, dims)


def product(left, right):
    top, rest = halves(right)
    return dot(left[0], top) + (dot(left[0], rest) + dot(left[1], top))


def chosen_slots(listed, slots):
    rows = lax.broadcasted_iota(jnp.int32, (slots, listed.shape[1]), 0)
    return (rows == listed).astype(F32).astype(BF16)


def traces_kernel(a_ref, lists_ref, low_ref, high_ref, face_ref):
    fields, nodes, slots = a_ref.shape
    face_ref[...] = jnp.zeros_like(face_ref)
    for f in range(fields):
        face_ref[0, pl.ds(f * FACE_NODES, FACE_NODES), :] = a_ref[f, 0:FACE_NODES, :]
        face_ref[1, pl.ds(f * FACE_NODES, FACE_NODES), :] = a_ref[f, nodes - FACE_NODES : nodes, :]
    low_ref[...] = pick(face_ref[0], chosen_slots(lists_ref[0:1, :], slots))
    high_ref[...] = pick(face_ref[1], chosen_slots(lists_ref[1:2, :], slots))


def operator_kernel(deriv_ref, mixing_ref, top_ref, rest_ref, sum_ref, pad_ref):
    directions, nodes, _ = deriv_ref.shape
    fields = top_ref.shape[0] // LANES
    pad_ref[...] = jnp.zeros_like(pad_ref)
    turned = []
    for d in range(directions):
        pad_ref[0:nodes, 0:nodes] = deriv_ref[d]
        turned.append(pad_ref[...].T)
    sum_ref[...] = functools.reduce(lambda a, b: a + b, turned)
    for f in range(fields):
        for g in range(fields):
            block = mixing_ref[g * fields + f] * turned[0]
            for d in range(1, directions):
                block = block + mixing_ref[(d * fields + g) * fields + f] * turned[d]
            top, rest = halves(block)
            top_ref[f * LANES : (f + 1) * LANES, g * LANES : (g + 1) * LANES] = top
            rest_ref[f * LANES : (f + 1) * LANES, g * LANES : (g + 1) * LANES] = rest


def outgoing_kernel(
    cap, major, minor, place_ref, a_ref, map_ref, lists_ref, low_ref, high_ref, near_low_ref,
    near_high_ref, *refs
):
    outs, (x_ref, f_ref, all_ref, turned_ref) = refs[:major], refs[major:]
    fields, nodes, slots = a_ref.shape
    wide = fields * LANES
    gain = step_size * face_gain
    all_ref[...] = jnp.zeros_like(all_ref)
    for f in range(fields):
        all_ref[pl.ds(f * LANES, nodes), :] = a_ref[f]
    all_ref[nodes : nodes + 1, :] = map_ref[...].astype(F32)
    x_ref[...] = all_ref[0:wide, :]
    low = pick(gain * (near_low_ref[...] - low_ref[...]), chosen_slots(lists_ref[0:1, :], slots), NT)
    high = pick(gain * (near_high_ref[...] - high_ref[...]), chosen_slots(lists_ref[1:2, :], slots), NT)
    all_ref[wide : wide + LANES, :] = low
    all_ref[wide + LANES : wide + 2 * LANES, :] = high
    f_ref[0:LANES, :] = low
    f_ref[LANES : 2 * LANES, :] = high
    turned_ref[...] = all_ref[...].T
    for j in range(major):
        s = lax.rem(place_ref[0] - j + major, major) * minor + place_ref[2]
        outs[j][...] = turned_ref[pl.ds(pl.multiple_of(s * cap, 8), cap), :]


def linear_kernel(nodes, x_ref, f_ref, top_ref, rest_ref, base_ref, face_ref, now_ref):
    wide = x_ref.shape[0]
    fields = wide // LANES
    op = (top_ref[...], rest_ref[...])
    x = x_ref[...]
    now_ref[...] = x + step_size * product(op, x)
    add_faces(now_ref, f_ref, fields, nodes)
    take_faces(now_ref, face_ref, fields, nodes)
    now = now_ref[...]
    base_ref[...] = now + step_size * product(op, now)


def add_faces(to_ref, face_ref, fields, nodes):
    for f in range(fields):
        at = f * LANES
        rows = f * FACE_NODES
        to_ref[pl.ds(at, FACE_NODES), :] += face_ref[pl.ds(rows, FACE_NODES), :]
        to_ref[pl.ds(at + nodes - FACE_NODES, FACE_NODES), :] += face_ref[
            pl.ds(LANES + rows, FACE_NODES), :
        ]


def take_faces(from_ref, face_ref, fields, nodes):
    face_ref[...] = jnp.zeros_like(face_ref)
    for f in range(fields):
        at = f * LANES
        rows = f * FACE_NODES
        face_ref[pl.ds(rows, FACE_NODES), :] = from_ref[pl.ds(at, FACE_NODES), :]
        face_ref[pl.ds(LANES + rows, FACE_NODES), :] = from_ref[
            pl.ds(at + nodes - FACE_NODES, FACE_NODES), :
        ]


def read_state(ref, segment, step, fields, nodes, f):
    parts = []
    halves_ = ref.shape[0] // (ref_segments(ref, fields, nodes) * fields * nodes * STEPS)
    stride = halves_ * STEPS
    for c in range(halves_):
        start = (segment * fields + f) * nodes * stride + c * STEPS + step
        parts.append(ref[pl.ds(start, nodes, stride=stride), :])
    return jnp.concatenate(parts, axis=1)


def ref_segments(ref, fields, nodes):
    return ref.shape[0] // (fields * nodes * STEPS * 2)


def advance(state_refs, weight_ref, step, a_ref, op, across_nodes, fields, nodes, q_ref, u_ref, sums_ref):
    elems = a_ref.shape[1]
    local = ref_segments(state_refs[0], fields, nodes)
    a = a_ref[...]
    linear = product(op, a)
    mean_state = None
    sums_ref[...] = jnp.zeros_like(sums_ref)
    density = jnp.zeros((1, elems), F32)
    u_ref[...] = jnp.zeros_like(u_ref)
    q_ref[...] = jnp.zeros_like(q_ref)
    for k, ref in enumerate(state_refs):
        for i in range(local):
            weight = weight_ref[k * local + i]
            for f in range(fields):
                u = read_state(ref, i, step, fields, nodes, f)
                u_ref[0:nodes, f * elems : (f + 1) * elems] = u
                q_ref[0:nodes, f * elems : (f + 1) * elems] = jnp.tanh(u)
            y = product(across_nodes, u_ref[...])
            p = jnp.zeros((LANES, elems), F32)
            r = jnp.zeros((LANES, elems), F32)
            line = jnp.zeros((LANES, elems), F32)
            for f in range(fields):
                q = q_ref[:, f * elems : (f + 1) * elems]
                p = p + q * a[f * LANES : (f + 1) * LANES, :]
                r = r + q * y[:, f * elems : (f + 1) * elems]
                line = line + u_ref[:, f * elems : (f + 1) * elems] * linear[f * LANES : (f + 1) * LANES, :]
            density = density + weight * jnp.sum(p * r + line, axis=0, keepdims=True)
            p = weight * p
            for f in range(fields):
                sums_ref[:, f * elems : (f + 1) * elems] += q_ref[:, f * elems : (f + 1) * elems] * p
    return linear, density


def slots_of(owner_ref, place_ref, cap, major, minor):
    elems = owner_ref.shape[1]
    owner = owner_ref[...]
    doms = -(-major * minor // 8) * 8
    rows = lax.broadcasted_iota(jnp.int32, (doms, elems), 0)
    named = (rows == owner).astype(F32)
    before = lax.broadcasted_iota(jnp.int32, (elems, elems), 0)
    after = lax.broadcasted_iota(jnp.int32, (elems, elems), 1)
    earlier = dot(named.astype(BF16), (before < after).astype(F32).astype(BF16))
    rank = jnp.sum(named * earlier, axis=0, keepdims=True).astype(jnp.int32)
    high = jnp.zeros_like(owner)
    for k in range(1, major):
        high = high + (owner >= k * minor).astype(jnp.int32)
    low = owner - high * minor
    high = high - place_ref[0]
    low = low - place_ref[2]
    high = jnp.where(high < 0, high + major, high)
    low = jnp.where(low < 0, low + minor, low)
    slot = (high * minor + low) * cap + rank
    return jnp.where(place_ref[3] > 0, slot, -1)


def product_all(total, sums_ref, linear, fields, elems):
    spread = product(total, sums_ref[...])
    return [
        linear[f * LANES : (f + 1) * LANES, :] + spread[:, f * elems : (f + 1) * elems]
        for f in range(fields)
    ]


def first_kernel(cap, major, minor, nodes, place_ref, weight_ref, owner_ref, top_ref, rest_ref, sum_ref, *refs):
    states = refs[:minor]
    blocks = refs[minor : minor + major * minor]
    refs = refs[minor + major * minor :]
    face_outs = refs[:major]
    now_ref, more_ref, got_ref, a_ref, fx_ref, q_ref, u_ref, sums_ref = refs[major:]
    elems = owner_ref.shape[1]
    slots = cap * major * minor
    wide = now_ref.shape[0]
    fields = wide // LANES
    slot = slots_of(owner_ref, place_ref, cap, major, minor)
    rows = lax.broadcasted_iota(jnp.int32, (slots, elems), 0)
    chosen = (rows == slot).astype(F32).astype(BF16)
    for n, block in enumerate(blocks):
        got_ref[n * cap : (n + 1) * cap, :] = block[...]
    here = pick(got_ref[...].T, chosen)
    a_ref[...] = here[0:wide]
    fx_ref[...] = here[wide:]
    param = here[nodes : nodes + 1, :]
    op = (top_ref[...], rest_ref[...])
    total = halves(sum_ref[...])
    across_nodes = halves(sum_ref[...].T)
    linear, density = advance(
        states, weight_ref, 0, a_ref, op, across_nodes, fields, nodes, q_ref, u_ref, sums_ref
    )
    volume = product_all(total, sums_ref, linear, fields, elems)
    for f in range(fields):
        now_ref[f * LANES : (f + 1) * LANES, :] = (
            a_ref[f * LANES : (f + 1) * LANES, :] + step_size * volume[f]
        )
    add_faces(now_ref, fx_ref, fields, nodes)
    take_faces(now_ref, fx_ref, fields, nodes)
    fx_ref[LANES - 3 : LANES - 2, :] = jnp.ones((1, elems), F32)
    sent = pick_back(chosen, fx_ref[...])
    width = cap * minor
    for k in range(major):
        face_outs[k][...] = sent[k * width : (k + 1) * width, :]
    more_ref[...] = jnp.concatenate(
        [density, param, slot.astype(F32), jnp.zeros((5, elems), F32)], axis=0
    )


def pick_back(chosen, value):
    top, rest = halves(value)
    return dot(chosen, top, NT) + dot(chosen, rest, NT)


def second_kernel(cap, major, minor, nodes, weight_ref, now_ref, more_ref, top_ref, rest_ref, sum_ref, *refs):
    states = refs[:minor]
    refs = refs[minor:]
    outs = refs[:major]
    grad_ref, t_ref, q_ref, u_ref, sums_ref = refs[major:]
    wide, elems = now_ref.shape
    fields = wide // LANES
    slots = cap * major * minor
    op = (top_ref[...], rest_ref[...])
    total = halves(sum_ref[...])
    across_nodes = halves(sum_ref[...].T)
    linear, density = advance(
        states, weight_ref, 1, now_ref, op, across_nodes, fields, nodes, q_ref, u_ref, sums_ref
    )
    volume = product_all(total, sums_ref, linear, fields, elems)
    for f in range(fields):
        t_ref[f * LANES : (f + 1) * LANES, :] = (
            now_ref[f * LANES : (f + 1) * LANES, :] + step_size * volume[f]
        )
    t_ref[nodes : nodes + 1, :] = jnp.ones((1, elems), F32)
    slot = more_ref[2:3, :].astype(jnp.int32)
    rows = lax.broadcasted_iota(jnp.int32, (slots, elems), 0)
    sent = pick_back((rows == slot).astype(F32).astype(BF16), t_ref[...])
    width = cap * minor
    for k in range(major):
        outs[k][...] = sent[k * width : (k + 1) * width, :]
    density = (more_ref[0:1, :] + density) * (1.0 / (fields * nodes))
    density = jnp.where(slot >= 0, density, 0.0)
    param = more_ref[1:2, :].astype(jnp.int32)
    count = PARAMS // LANES
    high = lax.shift_right_logical(param, 7)
    low = param - high * LANES
    in_high = lax.broadcasted_iota(jnp.int32, (count, elems), 0) == high
    in_low = (lax.broadcasted_iota(jnp.int32, (LANES, elems), 0) == low).astype(F32).astype(BF16)
    grad_ref[...] = pick(jnp.where(in_high, density, 0.0), in_low, NT)


def gathered(blocks, place_ref, got_ref, cap, major, minor):
    for j in range(major):
        for k in range(minor):
            s = lax.rem(place_ref[0] - j + major, major) * minor
            s = s + lax.rem(place_ref[1] - k + minor, minor)
            got_ref[pl.ds(pl.multiple_of(s * cap, 8), cap), :] = blocks[j * minor + k][...]


def faces_kernel(cap, major, minor, place_ref, base_ref, lists_ref, *refs):
    count = major * minor
    blocks = refs[:count]
    low_ref, high_ref, got_ref = refs[count:]
    gathered(blocks, place_ref, got_ref, cap, major, minor)
    slots = got_ref.shape[0]
    turned = got_ref[...].T
    mine = turned[LANES - 3 : LANES - 2, :] > 0.5
    now = jnp.where(mine, turned, base_ref[...])
    low_ref[...] = pick(now[0:LANES], chosen_slots(lists_ref[0:1, :], slots))
    high_ref[...] = pick(now[LANES:], chosen_slots(lists_ref[1:2, :], slots))


def last_kernel(
    cap, major, minor, place_ref, base_ref, lists_ref, low_ref, high_ref, near_low_ref, near_high_ref, *refs
):
    count = major * minor
    blocks = refs[:count]
    out_ref, got_ref, sum_ref, face_ref = refs[count:]
    fields, nodes, slots = out_ref.shape
    gain = step_size * face_gain
    gathered(blocks, place_ref, got_ref, cap, major, minor)
    turned = got_ref[...].T
    mine = turned[nodes : nodes + 1, :] > 0.5
    sum_ref[...] = jnp.where(mine, turned, base_ref[...])
    face_ref[0:LANES, :] = pick(
        gain * (near_low_ref[...] - low_ref[...]), chosen_slots(lists_ref[0:1, :], slots), NT
    )
    face_ref[LANES : 2 * LANES, :] = pick(
        gain * (near_high_ref[...] - high_ref[...]), chosen_slots(lists_ref[1:2, :], slots), NT
    )
    add_faces(sum_ref, face_ref, fields, nodes)
    for f in range(fields):
        out_ref[f] = sum_ref[pl.ds(f * LANES, nodes), :]


def across(low, high):
    size = lax.axis_size("region")
    up = [(i, i + 1) for i in range(size - 1)]
    near_low = lax.ppermute(high, "region", up)
    near_high = lax.ppermute(low, "region", [(j, i) for i, j in up])
    return near_low, near_high


def spread(parts, cap, major, minor):
    def at(sy, c, x):
        return (sy * minor + c) * minor + x

    axes = ("dom", "segment")
    moved = [parts[0]]
    for k in range(1, major):
        pairs = [(at(y, x, x), at((y + k) % major, x, x)) for y in range(major) for x in range(minor)]
        moved.append(lax.ppermute(parts[k], axes, pairs))
    blocks = []
    for part in moved:
        whole = part
        for k in range(1, minor):
            pairs = [(at(y, x, x), at(y, x, (x + k) % minor)) for y in range(major) for x in range(minor)]
            whole = whole + lax.ppermute(part, axes, pairs)
        blocks.append(whole[0:cap])
        for k in range(1, minor):
            pairs = [
                (at(y, c, x), at(y, (c + k) % minor, x))
                for y in range(major)
                for c in range(minor)
                for x in range(minor)
            ]
            blocks.append(lax.ppermute(whole[k * cap : (k + 1) * cap], axes, pairs))
    return blocks


def total_over(value, axis):
    size = lax.axis_size(axis)
    if size & (size - 1):
        return lax.psum(value, axis)
    k = 1
    while k < size:
        value = value + lax.ppermute(value, axis, [(i, i ^ k) for i in range(size)])
        k = 2 * k
    return value


def per_device(stored, new_owner, adjoint, deriv, mixing, face_lists, param_map):
    minor = lax.axis_size("segment")
    dom_count = lax.axis_size("dom")
    major = dom_count // minor
    local, _, fields, nodes, elems = stored.shape
    slots = adjoint.shape[2]
    faces = face_lists.shape[1]
    cap = slots // dom_count
    wide = fields * LANES
    axes = ("dom", "segment")

    def at(sy, c, x):
        return (sy * minor + c) * minor + x

    dom = lax.axis_index("dom")
    seg = lax.axis_index("segment")
    ty, tc = dom // minor, dom % minor
    place = jnp.stack([ty, tc, seg, (tc == seg).astype(jnp.int32)]).astype(jnp.int32)
    order = (seg + jnp.arange(minor, dtype=jnp.int32)) % minor
    table = jnp.array(rk_weights, F32).reshape(minor, local)
    weights = table[order].reshape(minor * local)
    owner = new_owner.reshape(1, elems)
    mapped = param_map.reshape(1, slots)

    rows = stored.reshape(local, STEPS, fields, nodes, elems // LANES, LANES)
    rows = rows.transpose(0, 2, 3, 4, 1, 5).reshape(-1, LANES)
    states = [rows]
    for k in range(1, minor):
        pairs = [
            (at(y, x, (x + k) % minor), at(y, x, x)) for y in range(major) for x in range(minor)
        ]
        states.append(lax.ppermute(rows, axes, pairs))

    trace = shape(LANES, faces)
    low, high = call(
        traces_kernel, (trace, trace), [VMEM, VMEM], [pltpu.VMEM((2, LANES, slots), F32)]
    )(adjoint, face_lists)
    near_low, near_high = across(low, high)
    top, rest, total = call(
        operator_kernel,
        (shape(wide, wide, dtype=BF16), shape(wide, wide, dtype=BF16), shape(LANES, LANES)),
        [VMEM, SMEM],
        [pltpu.VMEM((LANES, LANES), F32)],
    )(deriv, mixing.reshape(-1))

    sent = wide + 2 * LANES
    *outgoing, x, f0 = call(
        functools.partial(outgoing_kernel, cap, major, minor),
        (shape(cap, sent),) * major + (shape(wide, slots), shape(2 * LANES, slots)),
        [SMEM] + [VMEM] * 7,
        [pltpu.VMEM((sent, slots), F32), pltpu.VMEM((slots, sent), F32)],
    )(place, adjoint, mapped, face_lists, low, high, near_low, near_high)

    blocks = []
    for j in range(major):
        group = [outgoing[j]]
        for k in range(1, minor):
            pairs = [(at(y, (x + k) % minor, x), at(y, x, x)) for y in range(major) for x in range(minor)]
            group.append(lax.ppermute(outgoing[j], axes, pairs))
        if j:
            pairs = [(at((y + j) % major, x, x), at(y, x, x)) for y in range(major) for x in range(minor)]
            group = [lax.ppermute(g, axes, pairs) for g in group]
        blocks = blocks + group

    base, base_face = call(
        functools.partial(linear_kernel, nodes),
        (shape(wide, slots), shape(2 * LANES, slots)),
        [VMEM] * 4,
        [pltpu.VMEM((wide, slots), F32)],
        flops=2e9,
    )(x, f0, top, rest)

    width = cap * minor
    work = [
        pltpu.VMEM((LANES, fields * elems), F32),
        pltpu.VMEM((LANES, fields * elems), F32),
        pltpu.VMEM((LANES, fields * elems), F32),
    ]
    *face_parts, now, more = call(
        functools.partial(first_kernel, cap, major, minor, nodes),
        (shape(width, 2 * LANES),) * major + (shape(wide, elems), shape(8, elems)),
        [SMEM, SMEM] + [VMEM] * (4 + minor + dom_count),
        [
            pltpu.VMEM((slots, sent), F32),
            pltpu.VMEM((wide, elems), F32),
            pltpu.VMEM((2 * LANES, elems), F32),
        ]
        + work,
        flops=3e9,
    )(place, weights, owner, top, rest, total, *states, *blocks)
    face_blocks = spread(face_parts, cap, major, minor)

    *parts, grad = call(
        functools.partial(second_kernel, cap, major, minor, nodes),
        (shape(width, wide),) * major + (shape(PARAMS // LANES, LANES),),
        [SMEM] + [VMEM] * (5 + minor),
        [pltpu.VMEM((wide, elems), F32)] + work,
        flops=3e9,
    )(weights, now, more, top, rest, total, *states)
    last_blocks = spread(parts, cap, major, minor)

    low1, high1 = call(
        functools.partial(faces_kernel, cap, major, minor),
        (trace, trace),
        [SMEM] + [VMEM] * (2 + dom_count),
        [pltpu.VMEM((slots, 2 * LANES), F32)],
    )(place, base_face, face_lists, *face_blocks)
    near_low1, near_high1 = across(low1, high1)

    for axis in ("region", "dom", "segment"):
        grad = total_over(grad, axis)

    out = call(
        functools.partial(last_kernel, cap, major, minor),
        shape(fields, nodes, slots),
        [SMEM] + [VMEM] * (6 + dom_count),
        [
            pltpu.VMEM((slots, wide), F32),
            pltpu.VMEM((wide, slots), F32),
            pltpu.VMEM((2 * LANES, slots), F32),
        ],
    )(place, base, face_lists, low1, high1, near_low1, near_high1, *last_blocks)
    return (out, grad.reshape(PARAMS))


def solution(mesh):
    return jax.shard_map(
        per_device,
        mesh=mesh,
        in_specs=(
            P("segment", None, None, None, ("region", "dom")),
            P(("region", "dom"), None),
            P(None, None, ("region", "dom")),
            P(),
            P(),
            P(None, ("region", "dom")),
            P(("region", "dom")),
        ),
        out_specs=(P(None, None, ("region", "dom")), P()),
        check_vma=False,
    )
```

```python
import functools

import jax
import jax.numpy as jnp
from jax import lax
from jax.experimental import pallas as pl
from jax.experimental.pallas import tpu as pltpu
from jax.sharding import PartitionSpec as P

FACE_NODES = 25
STEPS = 2
PARAMS = 4096
LANES = 128
RIDE = PARAMS // (4 * LANES)

rk_weights = (1.0 / 6.0, 1.0 / 3.0, 1.0 / 3.0, 1.0 / 6.0)
step_size = 0.5
face_gain = 0.5

F32 = jnp.float32
BF16 = jnp.bfloat16
VMEM = pl.BlockSpec(memory_space=pltpu.VMEM)
SMEM = pl.BlockSpec(memory_space=pltpu.SMEM)
NN = (((1,), (0,)), ((), ()))
NT = (((1,), (1,)), ((), ()))


def call(body, outs, specs, scratch=(), flops=1e6, moved=1e4):
    return pl.pallas_call(
        body,
        out_shape=outs,
        in_specs=specs,
        out_specs=jax.tree.map(lambda _: VMEM, outs),
        scratch_shapes=list(scratch),
        compiler_params=pltpu.CompilerParams(vmem_limit_bytes=40 * 2**20),
        cost_estimate=pl.CostEstimate(
            flops=int(flops), bytes_accessed=int(moved), transcendentals=0
        ),
    )


def shape(*dims, dtype=F32):
    return jax.ShapeDtypeStruct(dims, dtype)


def halves(value):
    top = value.astype(BF16)
    return top, (value - top.astype(F32)).astype(BF16)


def dot(a, b, dims=NN):
    return lax.dot_general(a, b, dims, preferred_element_type=F32)


def pick(value, chosen, dims=NN):
    top, rest = halves(value)
    return dot(top, chosen, dims) + dot(rest, chosen, dims)


def product(left, right):
    top, rest = halves(right)
    return dot(left[0], top) + (dot(left[0], rest) + dot(left[1], top))


def chosen_slots(listed, slots):
    rows = lax.broadcasted_iota(jnp.int32, (slots, listed.shape[1]), 0)
    return (rows == listed).astype(F32).astype(BF16)


def stacked(value):
    top, rest = halves(value)
    return jnp.concatenate(
        [jnp.concatenate([top, top], axis=1), jnp.concatenate([rest, rest], axis=1)], axis=0
    )


def through(double, value):
    top, rest = halves(value)
    both = dot(double, jnp.concatenate([top, rest], axis=0))
    return both[:LANES] + both[LANES:]


def segment_weight(place_ref, minor, local, k, i):
    at = lax.rem(place_ref[2] + k, minor) * local + i
    weight = jnp.float32(rk_weights[0])
    for n in range(1, len(rk_weights)):
        weight = jnp.where(at == n, jnp.float32(rk_weights[n]), weight)
    return weight


def states_kernel(local, fields, nodes, rows_ref, *outs):
    parts = rows_ref.shape[0] // (local * fields * nodes * STEPS)
    stride = parts * STEPS
    for step in range(STEPS):
        for n in range(local * fields):
            for c in range(parts):
                start = n * nodes * stride + c * STEPS + step
                outs[step][n * LANES : n * LANES + nodes, c * LANES : (c + 1) * LANES] = rows_ref[
                    pl.ds(start, nodes, stride=stride), :
                ]
            outs[step][n * LANES + nodes : (n + 1) * LANES, :] = jnp.zeros(
                (LANES - nodes, parts * LANES), F32
            )


def start_kernel(place_ref, a_ref, lists_ref, one_ref, two_ref, face_ref):
    fields, nodes, slots = a_ref.shape
    face_ref[...] = jnp.zeros_like(face_ref)
    for f in range(fields):
        face_ref[0, pl.ds(f * FACE_NODES, FACE_NODES), :] = a_ref[f, 0:FACE_NODES, :]
        face_ref[1, pl.ds(f * FACE_NODES, FACE_NODES), :] = a_ref[f, nodes - FACE_NODES : nodes, :]
    low = pick(face_ref[0], chosen_slots(lists_ref[0:1, :], slots))
    high = pick(face_ref[1], chosen_slots(lists_ref[1:2, :], slots))
    put_traces(place_ref, low, high, one_ref, two_ref)


def put_traces(place_ref, low, high, one_ref, two_ref):
    even = place_ref[4] == 0
    one_ref[0:LANES, :] = jnp.where(even, high, low)
    two_ref[...] = jnp.where(even, low, high)


def face_rows(place_ref, lists_ref, one_ref, two_ref, near_one_ref, near_two_ref, slots, to_ref):
    gain = step_size * face_gain
    even = place_ref[4] == 0
    one = gain * (near_one_ref[0:LANES, :] - one_ref[0:LANES, :])
    two = gain * (near_two_ref[...] - two_ref[...])
    to_ref[0:LANES, :] = pick(
        jnp.where(even, two, one), chosen_slots(lists_ref[0:1, :], slots), NT
    )
    to_ref[LANES : 2 * LANES, :] = pick(
        jnp.where(even, one, two), chosen_slots(lists_ref[1:2, :], slots), NT
    )


def outgoing_kernel(
    cap, major, minor, place_ref, a_ref, map_ref, lists_ref, one_ref, two_ref, near_one_ref, near_two_ref, *refs
):
    outs, (f_ref, all_ref, turned_ref) = refs[:major], refs[major:]
    fields, nodes, slots = a_ref.shape
    wide = fields * LANES
    all_ref[0:wide, :] = jnp.zeros((wide, slots), F32)
    for f in range(fields):
        all_ref[pl.ds(f * LANES, nodes), :] = a_ref[f]
    all_ref[nodes : nodes + 1, :] = map_ref[...].astype(F32)
    face_rows(place_ref, lists_ref, one_ref, two_ref, near_one_ref, near_two_ref, slots, f_ref)
    all_ref[wide:, :] = f_ref[...]
    turned_ref[...] = all_ref[...].T
    for j in range(major):
        s = lax.rem(place_ref[0] - j + major, major) * minor + place_ref[2]
        outs[j][...] = turned_ref[pl.ds(pl.multiple_of(s * cap, 8), cap), :]


def operator_kernel(deriv_ref, mixing_ref, top_ref, rest_ref, sum_ref, pad_ref):
    directions, nodes, _ = deriv_ref.shape
    fields = top_ref.shape[0] // LANES
    pad_ref[...] = jnp.zeros_like(pad_ref)
    turned = []
    for d in range(directions):
        pad_ref[0:nodes, 0:nodes] = deriv_ref[d]
        turned.append(pad_ref[...].T)
    sum_ref[...] = functools.reduce(lambda a, b: a + b, turned)
    for f in range(fields):
        for g in range(fields):
            block = mixing_ref[g * fields + f] * turned[0]
            for d in range(1, directions):
                block = block + mixing_ref[(d * fields + g) * fields + f] * turned[d]
            top, rest = halves(block)
            top_ref[f * LANES : (f + 1) * LANES, g * LANES : (g + 1) * LANES] = top
            rest_ref[f * LANES : (f + 1) * LANES, g * LANES : (g + 1) * LANES] = rest


def linear_kernel(a_in_ref, f_ref, top_ref, rest_ref, base_ref, face_ref, now_ref, x_ref):
    fields, nodes, _ = a_in_ref.shape
    x_ref[...] = jnp.zeros_like(x_ref)
    for f in range(fields):
        x_ref[pl.ds(f * LANES, nodes), :] = a_in_ref[f]
    op = (top_ref[...], rest_ref[...])
    x = x_ref[...]
    now_ref[...] = x + step_size * product(op, x)
    add_faces(now_ref, f_ref, fields, nodes)
    take_faces(now_ref, face_ref, fields, nodes)
    now = now_ref[...]
    base_ref[...] = now + step_size * product(op, now)


def add_faces(to_ref, face_ref, fields, nodes):
    for f in range(fields):
        at = f * LANES
        rows = f * FACE_NODES
        to_ref[pl.ds(at, FACE_NODES), :] += face_ref[pl.ds(rows, FACE_NODES), :]
        to_ref[pl.ds(at + nodes - FACE_NODES, FACE_NODES), :] += face_ref[
            pl.ds(LANES + rows, FACE_NODES), :
        ]


def take_faces(from_ref, face_ref, fields, nodes):
    face_ref[...] = jnp.zeros_like(face_ref)
    for f in range(fields):
        at = f * LANES
        rows = f * FACE_NODES
        face_ref[pl.ds(rows, FACE_NODES), :] = from_ref[pl.ds(at, FACE_NODES), :]
        face_ref[pl.ds(LANES + rows, FACE_NODES), :] = from_ref[
            pl.ds(at + nodes - FACE_NODES, FACE_NODES), :
        ]


def ready_kernel(local, minor, place_ref, sum_ref, *refs):
    states, outs = refs[:STEPS], refs[STEPS:]
    fields = states[0].shape[0] // (local * LANES)
    double = stacked(sum_ref[...].T)
    for step in range(STEPS):
        for i in range(local):
            prepare(states[step], outs[2 * step], outs[2 * step + 1], double, segment_weight(place_ref, minor, local, 0, i), i, fields, i == 0)


def prepare(state_ref, r_ref, mean_ref, double, weight, i, fields, first):
    for f in range(fields):
        at = (i * fields + f) * LANES
        u = state_ref[at : at + LANES, :]
        part = jnp.tanh(u) * through(double, u)
        rows = slice(f * LANES, (f + 1) * LANES)
        if f == 0:
            r_ref[i * LANES : (i + 1) * LANES, :] = part
        else:
            r_ref[i * LANES : (i + 1) * LANES, :] += part
        if first:
            mean_ref[rows, :] = weight * u
        else:
            mean_ref[rows, :] += weight * u


def advance(minor, local, place_ref, states, r_ref, mean_ref, a_ref, op, sum_ref, t_ref, r_more_ref, mean_more_ref, q_ref, sums_ref):
    wide, elems = a_ref.shape
    fields = wide // LANES
    double = stacked(sum_ref[...].T)
    forward = stacked(sum_ref[...])
    linear = product(op, a_ref[...])
    dense = jnp.zeros((LANES, elems), F32)
    mean_more_ref[...] = mean_ref[...]
    for k in range(minor):
        for i in range(local):
            weight = segment_weight(place_ref, minor, local, k, i)
            if k:
                prepare(states[k], r_more_ref, mean_more_ref, double, weight, i, fields, False)
            r = (r_more_ref if k else r_ref)[i * LANES : (i + 1) * LANES, :]
            p = jnp.zeros((LANES, elems), F32)
            for f in range(fields):
                at = (i * fields + f) * LANES
                q = jnp.tanh(states[k][at : at + LANES, :])
                q_ref[f * LANES : (f + 1) * LANES, :] = q
                p = p + q * a_ref[f * LANES : (f + 1) * LANES, :]
            p = weight * p
            dense = dense + p * r
            for f in range(fields):
                rows = slice(f * LANES, (f + 1) * LANES)
                if k + i == 0:
                    sums_ref[rows, :] = q_ref[rows, :] * p
                else:
                    sums_ref[rows, :] += q_ref[rows, :] * p
    for f in range(fields):
        rows = slice(f * LANES, (f + 1) * LANES)
        dense = dense + linear[rows, :] * mean_more_ref[rows, :]
        volume = linear[rows, :] + through(forward, sums_ref[rows, :])
        t_ref[rows, :] = a_ref[rows, :] + step_size * volume
    return jnp.sum(dense, axis=0, keepdims=True)


def slots_of(owner_ref, place_ref, cap, major, minor):
    elems = owner_ref.shape[1]
    owner = owner_ref[...]
    doms = -(-major * minor // 8) * 8
    rows = lax.broadcasted_iota(jnp.int32, (doms, elems), 0)
    named = (rows == owner).astype(F32)
    before = lax.broadcasted_iota(jnp.int32, (elems, elems), 0)
    after = lax.broadcasted_iota(jnp.int32, (elems, elems), 1)
    earlier = dot(named.astype(BF16), (before < after).astype(F32).astype(BF16))
    rank = jnp.sum(named * earlier, axis=0, keepdims=True).astype(jnp.int32)
    high = jnp.zeros_like(owner)
    for k in range(1, major):
        high = high + (owner >= k * minor).astype(jnp.int32)
    low = owner - high * minor
    high = high - place_ref[0]
    low = low - place_ref[2]
    high = jnp.where(high < 0, high + major, high)
    low = jnp.where(low < 0, low + minor, low)
    slot = (high * minor + low) * cap + rank
    return jnp.where(place_ref[3] > 0, slot, -1)


def first_kernel(cap, major, minor, local, nodes, place_ref, owner_ref, top_ref, rest_ref, sum_ref, r_ref, mean_ref, *refs):
    states, refs = refs[:minor], refs[minor:]
    blocks, refs = refs[: major * minor], refs[major * minor :]
    now_ref, fx_ref, more_ref, got_ref, a_ref = refs[:5]
    elems = owner_ref.shape[1]
    slots = cap * major * minor
    wide = now_ref.shape[0]
    fields = wide // LANES
    slot = slots_of(owner_ref, place_ref, cap, major, minor)
    rows = lax.broadcasted_iota(jnp.int32, (slots, elems), 0)
    chosen = (rows == slot).astype(F32).astype(BF16)
    for n, block in enumerate(blocks):
        got_ref[n * cap : (n + 1) * cap, :] = block[...]
    here = pick(got_ref[...].T, chosen)
    a_ref[...] = here[0:wide]
    fx_ref[...] = here[wide:]
    param = a_ref[nodes : nodes + 1, :]
    op = (top_ref[...], rest_ref[...])
    density = advance(
        minor, local, place_ref, states, r_ref, mean_ref, a_ref, op, sum_ref, now_ref, *refs[5:]
    )
    add_faces(now_ref, fx_ref, fields, nodes)
    take_faces(now_ref, fx_ref, fields, nodes)
    fx_ref[LANES - 3 : LANES - 2, :] = jnp.ones((1, elems), F32)
    more_ref[...] = jnp.concatenate(
        [density, param, slot.astype(F32), jnp.zeros((5, elems), F32)], axis=0
    )


def pick_back(chosen, value):
    top, rest = halves(value)
    return dot(chosen, top, NT) + dot(chosen, rest, NT)


def second_kernel(cap, major, minor, local, nodes, place_ref, now_ref, faces_ref, more_ref, top_ref, rest_ref, sum_ref, r_ref, mean_ref, *refs):
    states, refs = refs[:minor], refs[minor:]
    outs, refs = refs[: major * minor], refs[major * minor :]
    t_ref = refs[0]
    wide, elems = now_ref.shape
    fields = wide // LANES
    slots = cap * major * minor
    op = (top_ref[...], rest_ref[...])
    density = advance(
        minor, local, place_ref, states, r_ref, mean_ref, now_ref, op, sum_ref, t_ref, *refs[1:]
    )
    t_ref[nodes : nodes + 1, :] = jnp.ones((1, elems), F32)
    slot = more_ref[2:3, :].astype(jnp.int32)
    rows = lax.broadcasted_iota(jnp.int32, (slots, elems), 0)
    chosen = (rows == slot).astype(F32).astype(BF16)
    sent = pick_back(chosen, t_ref[...])
    sent_faces = pick_back(chosen, faces_ref[...])
    density = (more_ref[0:1, :] + density) * (1.0 / (fields * nodes))
    density = jnp.where(slot >= 0, density, 0.0)
    param = more_ref[1:2, :].astype(jnp.int32)
    count = PARAMS // LANES
    high = lax.shift_right_logical(param, 7)
    low = param - high * LANES
    in_high = lax.broadcasted_iota(jnp.int32, (count, elems), 0) == high
    in_low = (lax.broadcasted_iota(jnp.int32, (LANES, elems), 0) == low).astype(F32).astype(BF16)
    grad = pick(jnp.where(in_high, density, 0.0), in_low, NT)
    for n, out in enumerate(outs):
        out[0:cap, 0:wide] = sent[n * cap : (n + 1) * cap, :]
        out[0:cap, wide:] = sent_faces[n * cap : (n + 1) * cap, :]
        out[cap : cap + RIDE, :] = jnp.zeros((RIDE, wide + 2 * LANES), F32)
        for m in range(4):
            out[cap : cap + RIDE, m * LANES : (m + 1) * LANES] = grad[m * RIDE : (m + 1) * RIDE, :]


def place_block(place_ref, got_ref, block, cap, major, minor, j, k):
    s = lax.rem(place_ref[0] - j + major, major) * minor
    s = s + lax.rem(place_ref[2] - k + minor, minor)
    got_ref[pl.ds(pl.multiple_of(s * cap, 8), cap), :] = block


def faces_kernel(cap, major, minor, place_ref, base_ref, lists_ref, *refs):
    one_ref, two_ref, got_ref = refs[minor:]
    for k in range(minor):
        for j in range(major):
            place_block(place_ref, got_ref, refs[k][j * cap : (j + 1) * cap, :], cap, major, minor, j, k)
    slots = got_ref.shape[0]
    turned = got_ref[...].T
    mine = turned[LANES - 3 : LANES - 2, :] > 0.5
    now = jnp.where(mine, turned, base_ref[...])
    low = pick(now[0:LANES], chosen_slots(lists_ref[0:1, :], slots))
    high = pick(now[LANES:], chosen_slots(lists_ref[1:2, :], slots))
    put_traces(place_ref, low, high, one_ref, two_ref)
    grad = refs[0][major * cap :, :]
    for k in range(1, minor):
        grad = grad + refs[k][major * cap :, :]
    for m in range(4):
        rows = slice(m // 2 * RIDE, (m // 2 + 1) * RIDE)
        at = LANES + m * RIDE
        one_ref[at : at + RIDE, :] = grad[rows, m % 2 * LANES : (m % 2 + 1) * LANES]


def assemble_kernel(nodes, cap, major, minor, place_ref, base_ref, *refs):
    count = major * minor
    out_ref, got_ref = refs[count:]
    for j in range(major):
        for k in range(minor):
            place_block(place_ref, got_ref, refs[j * minor + k][0:cap, :], cap, major, minor, j, k)
    turned = got_ref[...].T
    mine = turned[nodes : nodes + 1, :] > 0.5
    out_ref[...] = jnp.where(mine, turned, base_ref[...])


def last_kernel(place_ref, now_ref, lists_ref, one_ref, two_ref, near_one_ref, near_two_ref, out_ref, face_ref):
    fields, nodes, slots = out_ref.shape
    face_rows(place_ref, lists_ref, one_ref, two_ref, near_one_ref, near_two_ref, slots, face_ref)
    for f in range(fields):
        out_ref[f] = now_ref[pl.ds(f * LANES, nodes), :]
        rows = f * FACE_NODES
        out_ref[f, 0:FACE_NODES, :] += face_ref[pl.ds(rows, FACE_NODES), :]
        out_ref[f, nodes - FACE_NODES : nodes, :] += face_ref[pl.ds(LANES + rows, FACE_NODES), :]


def after(value, *earlier):
    return lax.optimization_barrier((value, *earlier))[0]


def across(one, two):
    size = lax.axis_size("region")
    near = []
    for value, first in ((one, 0), (two, 1)):
        pairs = [(i, i + 1) for i in range(first, size - 1, 2)]
        near.append(lax.ppermute(value, "region", pairs + [(j, i) for i, j in pairs]))
    return near


def summed_on(value, near, axis):
    size = lax.axis_size(axis)
    if size & (size - 1):
        return lax.psum(value, axis)
    value = value + near
    k = 2
    while k < size:
        value = value + lax.ppermute(value, axis, [(i, i ^ k) for i in range(size)])
        k = 2 * k
    return value


def per_device(stored, new_owner, adjoint, deriv, mixing, face_lists, param_map):
    minor = lax.axis_size("segment")
    dom_count = lax.axis_size("dom")
    major = dom_count // minor
    local, _, fields, nodes, elems = stored.shape
    slots = adjoint.shape[2]
    faces = face_lists.shape[1]
    cap = slots // dom_count
    wide = fields * LANES
    axes = ("dom", "segment")
    ys, xs = range(major), range(minor)

    def at(sy, c, x):
        return (sy * minor + c % minor) * minor + x % minor

    def move(value, pairs):
        return lax.ppermute(value, axes, pairs)

    def to_workers(parts):
        got = []
        for j in range(major):
            for k in range(minor):
                pairs = [(at((y + j) % major, x + k, x), at(y, x, x)) for y in ys for x in xs]
                got.append(move(parts[j], pairs) if j + k else parts[j])
        return got

    def from_workers(parts):
        got = []
        for j in range(major):
            total = None
            for k in range(minor):
                pairs = [(at(y, x, x), at((y + j) % major, x + k, x)) for y in ys for x in xs]
                part = parts[j * minor + k]
                part = move(part, pairs) if j + k else part
                total = part if total is None else total + part
            got.append(total)
        return got

    def to_segment(value, k):
        return lax.ppermute(value, "segment", [(x, (x + k) % minor) for x in xs])

    dom = lax.axis_index("dom")
    seg = lax.axis_index("segment")
    region = lax.axis_index("region")
    ty, tc = dom // minor, dom % minor
    place = jnp.stack([ty, tc, seg, (tc == seg).astype(jnp.int32), region % 2]).astype(jnp.int32)
    owner = new_owner.reshape(1, elems)
    mapped = param_map.reshape(1, slots)

    rows = stored.reshape(local, STEPS, fields, nodes, elems // LANES, LANES)
    rows = rows.transpose(0, 2, 3, 4, 1, 5).reshape(-1, LANES)
    own = call(
        functools.partial(states_kernel, local, fields, nodes),
        (shape(local * wide, elems),) * STEPS,
        [VMEM],
    )(rows)
    states = [
        [own[step]]
        + [
            lax.ppermute(
                own[step], axes, [(at(y, x, x + k), at(y, x, x)) for y in ys for x in xs]
            )
            for k in range(1, minor)
        ]
        for step in range(STEPS)
    ]

    trace = shape(LANES, faces)
    low, high = call(
        start_kernel,
        (trace, trace),
        [SMEM] + [VMEM] * 2,
        [pltpu.VMEM((2, LANES, slots), F32)],
    )(place, adjoint, face_lists)
    near_low, near_high = across(low, high)
    top, rest, total = call(
        operator_kernel,
        (shape(wide, wide, dtype=BF16), shape(wide, wide, dtype=BF16), shape(LANES, LANES)),
        [VMEM, SMEM],
        [pltpu.VMEM((LANES, LANES), F32)],
    )(deriv, mixing.reshape(-1))
    ready = call(
        functools.partial(ready_kernel, local, minor),
        (shape(local * LANES, elems), shape(wide, elems)) * STEPS,
        [SMEM] + [VMEM] * (1 + STEPS),
    )(place, total, *own)

    sent = wide + 2 * LANES
    *a_out, f0 = call(
        functools.partial(outgoing_kernel, cap, major, minor),
        (shape(cap, sent),) * major + (shape(2 * LANES, slots),),
        [SMEM] + [VMEM] * 7,
        [pltpu.VMEM((sent, slots), F32), pltpu.VMEM((slots, sent), F32)],
    )(place, adjoint, mapped, face_lists, low, high, near_low, near_high)
    blocks = to_workers(a_out)

    base, base_face = call(
        linear_kernel,
        (shape(wide, slots), shape(2 * LANES, slots)),
        [VMEM] * 4,
        [pltpu.VMEM((wide, slots), F32), pltpu.VMEM((wide, slots), F32)],
    )(adjoint, f0, top, rest)
    blocks[-1] = after(blocks[-1], base, base_face)

    work = [
        pltpu.VMEM((local * LANES, elems), F32),
        pltpu.VMEM((wide, elems), F32),
        pltpu.VMEM((wide, elems), F32),
        pltpu.VMEM((wide, elems), F32),
    ]
    now, faces_now, more = call(
        functools.partial(first_kernel, cap, major, minor, local, nodes),
        (shape(wide, elems), shape(2 * LANES, elems), shape(8, elems)),
        [SMEM] + [VMEM] * (6 + minor + dom_count),
        [
            pltpu.VMEM((slots, sent), F32),
            pltpu.VMEM((wide, elems), F32),
        ]
        + work,
    )(place, owner, top, rest, total, *ready[0:2], *states[0], *blocks)

    parts = call(
        functools.partial(second_kernel, cap, major, minor, local, nodes),
        (shape(cap + RIDE, sent),) * dom_count,
        [SMEM] + [VMEM] * (8 + minor),
        [pltpu.VMEM((wide, elems), F32)] + work,
    )(place, now, faces_now, more, top, rest, total, *ready[2:4], *states[1])
    got = from_workers(parts)
    last_blocks = []
    for value in got[:1]:
        mine = value[0:cap, 0:wide]
        last_blocks = last_blocks + [mine] + [to_segment(mine, k) for k in range(1, minor)]
    grad = sum(value[cap:, 0 : 4 * LANES] for value in got)
    mine = jnp.concatenate(
        [value[0:cap, wide:] for value in got] + [grad[:, 0 : 2 * LANES], grad[:, 2 * LANES :]]
    )
    face_blocks = [mine] + [to_segment(mine, k) for k in range(1, minor)]
    for value in got[1:]:
        mine = after(value[0:cap, 0:wide], last_blocks[-1])
        last_blocks = last_blocks + [mine] + [to_segment(mine, k) for k in range(1, minor)]
    low1, high1 = call(
        functools.partial(faces_kernel, cap, major, minor),
        (shape(LANES + 4 * RIDE, faces), trace),
        [SMEM] + [VMEM] * (2 + minor),
        [pltpu.VMEM((slots, 2 * LANES), F32)],
    )(place, base_face, face_lists, *face_blocks)
    near_low1, near_high1 = across(low1, high1)
    grad = summed_on(low1[LANES:], near_low1[LANES:], "region")

    assembled = call(
        functools.partial(assemble_kernel, nodes, cap, major, minor),
        shape(wide, slots),
        [SMEM] + [VMEM] * (1 + dom_count),
        [pltpu.VMEM((slots, wide), F32)],
        moved=8e7,
    )(place, base, *last_blocks)
    out = call(
        last_kernel,
        shape(fields, nodes, slots),
        [SMEM] + [VMEM] * 6,
        [pltpu.VMEM((2 * LANES, slots), F32)],
    )(place, assembled, face_lists, low1, high1, near_low1, near_high1)
    return (out, grad.reshape(PARAMS))


def solution(mesh):
    return jax.shard_map(
        per_device,
        mesh=mesh,
        in_specs=(
            P("segment", None, None, None, ("region", "dom")),
            P(("region", "dom"), None),
            P(None, None, ("region", "dom")),
            P(),
            P(),
            P(None, ("region", "dom")),
            P(("region", "dom")),
        ),
        out_specs=(P(None, None, ("region", "dom")), P()),
        check_vma=False,
    )
```

```python
import functools

import jax
import jax.numpy as jnp
from jax import lax
from jax.experimental import pallas as pl
from jax.experimental.pallas import tpu as pltpu
from jax.sharding import PartitionSpec as P

FACE_NODES = 25
STEPS = 2
PARAMS = 4096
LANES = 128
RIDE = PARAMS // (4 * LANES)

rk_weights = (1.0 / 6.0, 1.0 / 3.0, 1.0 / 3.0, 1.0 / 6.0)
step_size = 0.5
face_gain = 0.5

F32 = jnp.float32
BF16 = jnp.bfloat16
VMEM = pl.BlockSpec(memory_space=pltpu.VMEM)
SMEM = pl.BlockSpec(memory_space=pltpu.SMEM)
NN = (((1,), (0,)), ((), ()))
NT = (((1,), (1,)), ((), ()))


def call(body, outs, specs, scratch=(), flops=1e6, moved=1e4):
    return pl.pallas_call(
        body,
        out_shape=outs,
        in_specs=specs,
        out_specs=jax.tree.map(lambda _: VMEM, outs),
        scratch_shapes=list(scratch),
        compiler_params=pltpu.CompilerParams(vmem_limit_bytes=40 * 2**20),
        cost_estimate=pl.CostEstimate(
            flops=int(flops), bytes_accessed=int(moved), transcendentals=0
        ),
    )


def shape(*dims, dtype=F32):
    return jax.ShapeDtypeStruct(dims, dtype)


def halves(value):
    top = value.astype(BF16)
    return top, (value - top.astype(F32)).astype(BF16)


def dot(a, b, dims=NN):
    return lax.dot_general(a, b, dims, preferred_element_type=F32)


def pick(value, chosen, dims=NN):
    top, rest = halves(value)
    return dot(top, chosen, dims) + dot(rest, chosen, dims)


def product(left, right):
    top, rest = halves(right)
    return dot(left[0], top) + (dot(left[0], rest) + dot(left[1], top))


def chosen_slots(listed, slots):
    rows = lax.broadcasted_iota(jnp.int32, (slots, listed.shape[1]), 0)
    return (rows == listed).astype(F32).astype(BF16)


def stacked(value):
    top, rest = halves(value)
    return jnp.concatenate(
        [jnp.concatenate([top, top], axis=1), jnp.concatenate([rest, rest], axis=1)], axis=0
    )


def through(double, value):
    top, rest = halves(value)
    both = dot(double, jnp.concatenate([top, rest], axis=0))
    return both[:LANES] + both[LANES:]


def segment_weight(place_ref, minor, local, k, i):
    at = lax.rem(place_ref[2] + k, minor) * local + i
    weight = jnp.float32(rk_weights[0])
    for n in range(1, len(rk_weights)):
        weight = jnp.where(at == n, jnp.float32(rk_weights[n]), weight)
    return weight


def states_kernel(local, fields, nodes, rows_ref, *outs):
    parts = rows_ref.shape[0] // (local * fields * nodes * STEPS)
    stride = parts * STEPS
    for step in range(STEPS):
        for n in range(local * fields):
            for c in range(parts):
                start = n * nodes * stride + c * STEPS + step
                outs[step][n * LANES : n * LANES + nodes, c * LANES : (c + 1) * LANES] = rows_ref[
                    pl.ds(start, nodes, stride=stride), :
                ]
            outs[step][n * LANES + nodes : (n + 1) * LANES, :] = jnp.zeros(
                (LANES - nodes, parts * LANES), F32
            )


def start_kernel(place_ref, a_ref, lists_ref, one_ref, two_ref, face_ref):
    fields, nodes, slots = a_ref.shape
    face_ref[...] = jnp.zeros_like(face_ref)
    for f in range(fields):
        face_ref[0, pl.ds(f * FACE_NODES, FACE_NODES), :] = a_ref[f, 0:FACE_NODES, :]
        face_ref[1, pl.ds(f * FACE_NODES, FACE_NODES), :] = a_ref[f, nodes - FACE_NODES : nodes, :]
    low = pick(face_ref[0], chosen_slots(lists_ref[0:1, :], slots))
    high = pick(face_ref[1], chosen_slots(lists_ref[1:2, :], slots))
    put_traces(place_ref, low, high, one_ref, two_ref)


def put_traces(place_ref, low, high, one_ref, two_ref):
    even = place_ref[4] == 0
    one_ref[0:LANES, :] = jnp.where(even, high, low)
    two_ref[0:LANES, :] = jnp.where(even, low, high)


def face_rows(place_ref, lists_ref, one_ref, two_ref, near_one_ref, near_two_ref, slots, to_ref):
    gain = step_size * face_gain
    even = place_ref[4] == 0
    one = gain * (near_one_ref[0:LANES, :] - one_ref[0:LANES, :])
    near_two = jnp.where(place_ref[5] > 0, near_two_ref[0:LANES, :], 0.0)
    two = gain * (near_two - two_ref[0:LANES, :])
    to_ref[0:LANES, :] = pick(
        jnp.where(even, two, one), chosen_slots(lists_ref[0:1, :], slots), NT
    )
    to_ref[LANES : 2 * LANES, :] = pick(
        jnp.where(even, one, two), chosen_slots(lists_ref[1:2, :], slots), NT
    )


def outgoing_kernel(
    cap, major, minor, place_ref, a_ref, map_ref, lists_ref, one_ref, two_ref, near_one_ref, near_two_ref, *refs
):
    outs, (f_ref, all_ref, turned_ref) = refs[:major], refs[major:]
    fields, nodes, slots = a_ref.shape
    wide = fields * LANES
    all_ref[0:wide, :] = jnp.zeros((wide, slots), F32)
    for f in range(fields):
        all_ref[pl.ds(f * LANES, nodes), :] = a_ref[f]
    all_ref[nodes : nodes + 1, :] = map_ref[...].astype(F32)
    face_rows(place_ref, lists_ref, one_ref, two_ref, near_one_ref, near_two_ref, slots, f_ref)
    all_ref[wide:, :] = f_ref[...]
    turned_ref[...] = all_ref[...].T
    for j in range(major):
        s = lax.rem(place_ref[0] - j + major, major) * minor + place_ref[2]
        outs[j][...] = turned_ref[pl.ds(pl.multiple_of(s * cap, 8), cap), :]


def operator_kernel(deriv_ref, mixing_ref, top_ref, rest_ref, sum_ref, pad_ref):
    directions, nodes, _ = deriv_ref.shape
    fields = top_ref.shape[0] // LANES
    pad_ref[...] = jnp.zeros_like(pad_ref)
    turned = []
    for d in range(directions):
        pad_ref[0:nodes, 0:nodes] = deriv_ref[d]
        turned.append(pad_ref[...].T)
    sum_ref[...] = functools.reduce(lambda a, b: a + b, turned)
    for f in range(fields):
        for g in range(fields):
            block = mixing_ref[g * fields + f] * turned[0]
            for d in range(1, directions):
                block = block + mixing_ref[(d * fields + g) * fields + f] * turned[d]
            top, rest = halves(block)
            top_ref[f * LANES : (f + 1) * LANES, g * LANES : (g + 1) * LANES] = top
            rest_ref[f * LANES : (f + 1) * LANES, g * LANES : (g + 1) * LANES] = rest


def linear_kernel(a_in_ref, f_ref, top_ref, rest_ref, base_ref, face_ref, now_ref, x_ref):
    fields, nodes, _ = a_in_ref.shape
    x_ref[...] = jnp.zeros_like(x_ref)
    for f in range(fields):
        x_ref[pl.ds(f * LANES, nodes), :] = a_in_ref[f]
    op = (top_ref[...], rest_ref[...])
    x = x_ref[...]
    now_ref[...] = x + step_size * product(op, x)
    add_faces(now_ref, f_ref, fields, nodes)
    take_faces(now_ref, face_ref, fields, nodes)
    now = now_ref[...]
    base_ref[...] = now + step_size * product(op, now)


def add_faces(to_ref, face_ref, fields, nodes):
    for f in range(fields):
        at = f * LANES
        rows = f * FACE_NODES
        to_ref[pl.ds(at, FACE_NODES), :] += face_ref[pl.ds(rows, FACE_NODES), :]
        to_ref[pl.ds(at + nodes - FACE_NODES, FACE_NODES), :] += face_ref[
            pl.ds(LANES + rows, FACE_NODES), :
        ]


def take_faces(from_ref, face_ref, fields, nodes):
    face_ref[...] = jnp.zeros_like(face_ref)
    for f in range(fields):
        at = f * LANES
        rows = f * FACE_NODES
        face_ref[pl.ds(rows, FACE_NODES), :] = from_ref[pl.ds(at, FACE_NODES), :]
        face_ref[pl.ds(LANES + rows, FACE_NODES), :] = from_ref[
            pl.ds(at + nodes - FACE_NODES, FACE_NODES), :
        ]


def ready_kernel(local, minor, place_ref, sum_ref, *refs):
    states, outs = refs[:STEPS], refs[STEPS:]
    fields = states[0].shape[0] // (local * LANES)
    double = stacked(sum_ref[...].T)
    for step in range(STEPS):
        for i in range(local):
            prepare(states[step], outs[2 * step], outs[2 * step + 1], double, segment_weight(place_ref, minor, local, 0, i), i, fields, i == 0)


def prepare(state_ref, r_ref, mean_ref, double, weight, i, fields, first):
    for f in range(fields):
        at = (i * fields + f) * LANES
        u = state_ref[at : at + LANES, :]
        part = jnp.tanh(u) * through(double, u)
        rows = slice(f * LANES, (f + 1) * LANES)
        if f == 0:
            r_ref[i * LANES : (i + 1) * LANES, :] = part
        else:
            r_ref[i * LANES : (i + 1) * LANES, :] += part
        if first:
            mean_ref[rows, :] = weight * u
        else:
            mean_ref[rows, :] += weight * u


def advance(minor, local, place_ref, states, r_ref, mean_ref, a_ref, op, sum_ref, t_ref, r_more_ref, mean_more_ref, q_ref, sums_ref):
    wide, elems = a_ref.shape
    fields = wide // LANES
    double = stacked(sum_ref[...].T)
    forward = stacked(sum_ref[...])
    linear = product(op, a_ref[...])
    dense = jnp.zeros((LANES, elems), F32)
    mean_more_ref[...] = mean_ref[...]
    for k in range(minor):
        for i in range(local):
            weight = segment_weight(place_ref, minor, local, k, i)
            if k:
                prepare(states[k], r_more_ref, mean_more_ref, double, weight, i, fields, False)
            r = (r_more_ref if k else r_ref)[i * LANES : (i + 1) * LANES, :]
            p = jnp.zeros((LANES, elems), F32)
            for f in range(fields):
                at = (i * fields + f) * LANES
                q = jnp.tanh(states[k][at : at + LANES, :])
                q_ref[f * LANES : (f + 1) * LANES, :] = q
                p = p + q * a_ref[f * LANES : (f + 1) * LANES, :]
            p = weight * p
            dense = dense + p * r
            for f in range(fields):
                rows = slice(f * LANES, (f + 1) * LANES)
                if k + i == 0:
                    sums_ref[rows, :] = q_ref[rows, :] * p
                else:
                    sums_ref[rows, :] += q_ref[rows, :] * p
    for f in range(fields):
        rows = slice(f * LANES, (f + 1) * LANES)
        dense = dense + linear[rows, :] * mean_more_ref[rows, :]
        volume = linear[rows, :] + through(forward, sums_ref[rows, :])
        t_ref[rows, :] = a_ref[rows, :] + step_size * volume
    return jnp.sum(dense, axis=0, keepdims=True)


def slots_of(owner_ref, place_ref, cap, major, minor):
    elems = owner_ref.shape[1]
    owner = owner_ref[...]
    doms = -(-major * minor // 8) * 8
    rows = lax.broadcasted_iota(jnp.int32, (doms, elems), 0)
    named = (rows == owner).astype(F32)
    before = lax.broadcasted_iota(jnp.int32, (elems, elems), 0)
    after = lax.broadcasted_iota(jnp.int32, (elems, elems), 1)
    earlier = dot(named.astype(BF16), (before < after).astype(F32).astype(BF16))
    rank = jnp.sum(named * earlier, axis=0, keepdims=True).astype(jnp.int32)
    high = jnp.zeros_like(owner)
    for k in range(1, major):
        high = high + (owner >= k * minor).astype(jnp.int32)
    low = owner - high * minor
    high = high - place_ref[0]
    low = low - place_ref[2]
    high = jnp.where(high < 0, high + major, high)
    low = jnp.where(low < 0, low + minor, low)
    slot = (high * minor + low) * cap + rank
    return jnp.where(place_ref[3] > 0, slot, -1)


def first_kernel(cap, major, minor, local, nodes, place_ref, owner_ref, top_ref, rest_ref, sum_ref, r_ref, mean_ref, *refs):
    states, refs = refs[:minor], refs[minor:]
    blocks, refs = refs[: major * minor], refs[major * minor :]
    face_outs, refs = refs[:major], refs[major:]
    now_ref, more_ref, got_ref, a_ref, fx_ref = refs[:5]
    elems = owner_ref.shape[1]
    slots = cap * major * minor
    wide = now_ref.shape[0]
    fields = wide // LANES
    slot = slots_of(owner_ref, place_ref, cap, major, minor)
    rows = lax.broadcasted_iota(jnp.int32, (slots, elems), 0)
    chosen = (rows == slot).astype(F32).astype(BF16)
    for n, block in enumerate(blocks):
        got_ref[n * cap : (n + 1) * cap, :] = block[...]
    here = pick(got_ref[...].T, chosen)
    a_ref[...] = here[0:wide]
    fx_ref[...] = here[wide:]
    param = a_ref[nodes : nodes + 1, :]
    op = (top_ref[...], rest_ref[...])
    density = advance(
        minor, local, place_ref, states, r_ref, mean_ref, a_ref, op, sum_ref, now_ref, *refs[5:]
    )
    add_faces(now_ref, fx_ref, fields, nodes)
    take_faces(now_ref, fx_ref, fields, nodes)
    fx_ref[LANES - 3 : LANES - 2, :] = jnp.ones((1, elems), F32)
    sent = pick_back(chosen, fx_ref[...])
    width = cap * minor
    for k in range(major):
        face_outs[k][...] = sent[k * width : (k + 1) * width, :]
    more_ref[...] = jnp.concatenate(
        [density, param, slot.astype(F32), jnp.zeros((5, elems), F32)], axis=0
    )


def pick_back(chosen, value):
    top, rest = halves(value)
    return dot(chosen, top, NT) + dot(chosen, rest, NT)


def second_kernel(cap, major, minor, local, nodes, place_ref, now_ref, more_ref, top_ref, rest_ref, sum_ref, r_ref, mean_ref, *refs):
    states, refs = refs[:minor], refs[minor:]
    outs, refs = refs[: major * minor], refs[major * minor :]
    t_ref = refs[0]
    wide, elems = now_ref.shape
    fields = wide // LANES
    slots = cap * major * minor
    op = (top_ref[...], rest_ref[...])
    density = advance(
        minor, local, place_ref, states, r_ref, mean_ref, now_ref, op, sum_ref, t_ref, *refs[1:]
    )
    t_ref[nodes : nodes + 1, :] = jnp.ones((1, elems), F32)
    slot = more_ref[2:3, :].astype(jnp.int32)
    rows = lax.broadcasted_iota(jnp.int32, (slots, elems), 0)
    chosen = (rows == slot).astype(F32).astype(BF16)
    sent = pick_back(chosen, t_ref[...])
    density = (more_ref[0:1, :] + density) * (1.0 / (fields * nodes))
    density = jnp.where(slot >= 0, density, 0.0)
    param = more_ref[1:2, :].astype(jnp.int32)
    count = PARAMS // LANES
    high = lax.shift_right_logical(param, 7)
    low = param - high * LANES
    in_high = lax.broadcasted_iota(jnp.int32, (count, elems), 0) == high
    in_low = (lax.broadcasted_iota(jnp.int32, (LANES, elems), 0) == low).astype(F32).astype(BF16)
    grad = pick(jnp.where(in_high, density, 0.0), in_low, NT)
    for n, out in enumerate(outs):
        out[0:cap, 0:wide] = sent[n * cap : (n + 1) * cap, :]
        out[cap : cap + RIDE, :] = jnp.zeros((RIDE, wide), F32)
        for m in range(4):
            out[cap : cap + RIDE, m * LANES : (m + 1) * LANES] = grad[m * RIDE : (m + 1) * RIDE, :]


def place_block(place_ref, got_ref, block, cap, major, minor, j, k):
    s = lax.rem(place_ref[0] - j + major, major) * minor
    s = s + lax.rem(place_ref[2] - k + minor, minor)
    got_ref[pl.ds(pl.multiple_of(s * cap, 8), cap), :] = block


def faces_kernel(cap, major, minor, place_ref, base_ref, lists_ref, *refs):
    one_ref, two_ref, got_ref = refs[minor:]
    for k in range(minor):
        for j in range(major):
            place_block(place_ref, got_ref, refs[k][j * cap : (j + 1) * cap, :], cap, major, minor, j, k)
    slots = got_ref.shape[0]
    turned = got_ref[...].T
    mine = turned[LANES - 3 : LANES - 2, :] > 0.5
    now = jnp.where(mine, turned, base_ref[...])
    low = pick(now[0:LANES], chosen_slots(lists_ref[0:1, :], slots))
    high = pick(now[LANES:], chosen_slots(lists_ref[1:2, :], slots))
    put_traces(place_ref, low, high, one_ref, two_ref)
    grad = refs[0][major * cap :, :]
    for k in range(1, minor):
        grad = grad + refs[k][major * cap :, :]
    for m in range(4):
        rows = slice(m // 2 * RIDE, (m // 2 + 1) * RIDE)
        at = LANES + m * RIDE
        part = grad[rows, m % 2 * LANES : (m % 2 + 1) * LANES]
        one_ref[at : at + RIDE, :] = part
        two_ref[at : at + RIDE, :] = part


def assemble_kernel(nodes, cap, major, minor, place_ref, base_ref, *refs):
    out_ref, got_ref = refs[minor:]
    for k in range(minor):
        for j in range(major):
            place_block(place_ref, got_ref, refs[k][j * cap : (j + 1) * cap, :], cap, major, minor, j, k)
    turned = got_ref[...].T
    mine = turned[nodes : nodes + 1, :] > 0.5
    out_ref[...] = jnp.where(mine, turned, base_ref[...])


def last_kernel(place_ref, now_ref, lists_ref, one_ref, two_ref, near_one_ref, near_two_ref, out_ref, face_ref):
    fields, nodes, slots = out_ref.shape
    face_rows(place_ref, lists_ref, one_ref, two_ref, near_one_ref, near_two_ref, slots, face_ref)
    for f in range(fields):
        out_ref[f] = now_ref[pl.ds(f * LANES, nodes), :]
        rows = f * FACE_NODES
        out_ref[f, 0:FACE_NODES, :] += face_ref[pl.ds(rows, FACE_NODES), :]
        out_ref[f, nodes - FACE_NODES : nodes, :] += face_ref[pl.ds(LANES + rows, FACE_NODES), :]


def after(value, *earlier):
    return lax.optimization_barrier((value, *earlier))[0]


def across(one, two, ends):
    size = lax.axis_size("region")
    near = []
    for value, first in ((one, 0), (two, 1)):
        pairs = [(i, i + 1) for i in range(first, size - 1, 2)]
        if ends and first and size == 4:
            pairs = pairs + [(0, 3)]
        near.append(lax.ppermute(value, "region", pairs + [(j, i) for i, j in pairs]))
    return near


def over_regions(value, near_one, near_two):
    size = lax.axis_size("region")
    if size == 4:
        far = lax.ppermute(value, "region", [(i, i ^ 2) for i in range(size)])
        return (value + near_one) + (near_two + far)
    return lax.psum(value, "region")


def per_device(stored, new_owner, adjoint, deriv, mixing, face_lists, param_map):
    minor = lax.axis_size("segment")
    dom_count = lax.axis_size("dom")
    major = dom_count // minor
    local, _, fields, nodes, elems = stored.shape
    slots = adjoint.shape[2]
    faces = face_lists.shape[1]
    cap = slots // dom_count
    wide = fields * LANES
    axes = ("dom", "segment")
    ys, xs = range(major), range(minor)

    def at(sy, c, x):
        return (sy * minor + c % minor) * minor + x % minor

    def move(value, pairs):
        return lax.ppermute(value, axes, pairs)

    def to_workers(parts):
        got = []
        for j in range(major):
            for k in range(minor):
                pairs = [(at((y + j) % major, x + k, x), at(y, x, x)) for y in ys for x in xs]
                got.append(move(parts[j], pairs) if j + k else parts[j])
        return got

    def from_workers(parts):
        got = []
        for j in range(major):
            total = None
            for k in range(minor):
                pairs = [(at(y, x, x), at((y + j) % major, x + k, x)) for y in ys for x in xs]
                part = parts[j * minor + k]
                part = move(part, pairs) if j + k else part
                total = part if total is None else total + part
            got.append(total)
        return got

    def to_segment(value, k):
        return lax.ppermute(value, "segment", [(x, (x + k) % minor) for x in xs])

    dom = lax.axis_index("dom")
    seg = lax.axis_index("segment")
    region = lax.axis_index("region")
    size = lax.axis_size("region")
    second = 1 - ((region == 0) | ((region == size - 1) & (size % 2 == 0))).astype(jnp.int32)
    ty, tc = dom // minor, dom % minor
    place = jnp.stack([ty, tc, seg, (tc == seg).astype(jnp.int32), region % 2, second]).astype(jnp.int32)
    owner = new_owner.reshape(1, elems)
    mapped = param_map.reshape(1, slots)

    rows = stored.reshape(local, STEPS, fields, nodes, elems // LANES, LANES)
    rows = rows.transpose(0, 2, 3, 4, 1, 5).reshape(-1, LANES)
    own = call(
        functools.partial(states_kernel, local, fields, nodes),
        (shape(local * wide, elems),) * STEPS,
        [VMEM],
    )(rows)
    states = [
        [own[step]]
        + [
            lax.ppermute(
                own[step], axes, [(at(y, x, x + k), at(y, x, x)) for y in ys for x in xs]
            )
            for k in range(1, minor)
        ]
        for step in range(STEPS)
    ]

    trace = shape(LANES, faces)
    low, high = call(
        start_kernel,
        (trace, trace),
        [SMEM] + [VMEM] * 2,
        [pltpu.VMEM((2, LANES, slots), F32)],
    )(place, adjoint, face_lists)
    near_low, near_high = across(low, high, False)
    top, rest, total = call(
        operator_kernel,
        (shape(wide, wide, dtype=BF16), shape(wide, wide, dtype=BF16), shape(LANES, LANES)),
        [VMEM, SMEM],
        [pltpu.VMEM((LANES, LANES), F32)],
    )(deriv, mixing.reshape(-1))
    ready = call(
        functools.partial(ready_kernel, local, minor),
        (shape(local * LANES, elems), shape(wide, elems)) * STEPS,
        [SMEM] + [VMEM] * (1 + STEPS),
    )(place, total, *own)

    sent = wide + 2 * LANES
    *a_out, f0 = call(
        functools.partial(outgoing_kernel, cap, major, minor),
        (shape(cap, sent),) * major + (shape(2 * LANES, slots),),
        [SMEM] + [VMEM] * 7,
        [pltpu.VMEM((sent, slots), F32), pltpu.VMEM((slots, sent), F32)],
    )(place, adjoint, mapped, face_lists, low, high, near_low, near_high)
    blocks = to_workers(a_out)

    base, base_face = call(
        linear_kernel,
        (shape(wide, slots), shape(2 * LANES, slots)),
        [VMEM] * 4,
        [pltpu.VMEM((wide, slots), F32), pltpu.VMEM((wide, slots), F32)],
    )(adjoint, f0, top, rest)
    blocks[-1] = after(blocks[-1], base, base_face)

    work = [
        pltpu.VMEM((local * LANES, elems), F32),
        pltpu.VMEM((wide, elems), F32),
        pltpu.VMEM((wide, elems), F32),
        pltpu.VMEM((wide, elems), F32),
    ]
    *face_parts, now, more = call(
        functools.partial(first_kernel, cap, major, minor, local, nodes),
        (shape(cap * minor, 2 * LANES),) * major + (shape(wide, elems), shape(8, elems)),
        [SMEM] + [VMEM] * (6 + minor + dom_count),
        [
            pltpu.VMEM((slots, sent), F32),
            pltpu.VMEM((wide, elems), F32),
            pltpu.VMEM((2 * LANES, elems), F32),
        ]
        + work,
    )(place, owner, top, rest, total, *ready[0:2], *states[0], *blocks)

    moved = [face_parts[0]] + [
        move(face_parts[j], [(at(y, x, x), at((y + j) % major, x, x)) for y in ys for x in xs])
        for j in range(1, major)
    ]
    parts = call(
        functools.partial(second_kernel, cap, major, minor, local, nodes),
        (shape(cap + RIDE, wide),) * dom_count,
        [SMEM] + [VMEM] * (7 + minor),
        [pltpu.VMEM((wide, elems), F32)] + work,
        moved=4e7,
    )(place, now, more, top, rest, total, *ready[2:4], *states[1])
    moved[-1] = after(moved[-1], *parts)
    joined = [
        jnp.concatenate([part[k * cap : (k + 1) * cap] for part in moved]) for k in range(minor)
    ]
    faces_mine = joined[0]
    for k in range(1, minor):
        pairs = [(at(y, x, x), at(y, x + k, x)) for y in ys for x in xs]
        faces_mine = faces_mine + move(joined[k], pairs)
    got = from_workers(parts)
    grad = sum(value[cap:, 0 : 4 * LANES] for value in got)
    mine = jnp.concatenate([faces_mine, grad[:, 0 : 2 * LANES], grad[:, 2 * LANES :]])
    face_blocks = [mine] + [to_segment(mine, k) for k in range(1, minor)]
    mine = jnp.concatenate([value[0:cap] for value in got])
    last_blocks = [mine] + [to_segment(mine, k) for k in range(1, minor)]
    face_blocks[-1] = after(face_blocks[-1], mine)
    low1, high1 = call(
        functools.partial(faces_kernel, cap, major, minor),
        (shape(LANES + 4 * RIDE, faces),) * 2,
        [SMEM] + [VMEM] * (2 + minor),
        [pltpu.VMEM((slots, 2 * LANES), F32)],
    )(place, base_face, face_lists, *face_blocks)
    near_low1, near_high1 = across(low1, high1, True)
    grad = over_regions(low1[LANES:], near_low1[LANES:], near_high1[LANES:])

    assembled = call(
        functools.partial(assemble_kernel, nodes, cap, major, minor),
        shape(wide, slots),
        [SMEM] + [VMEM] * (1 + minor),
        [pltpu.VMEM((slots, wide), F32)],
        moved=8e7,
    )(place, base, *last_blocks)
    out = call(
        last_kernel,
        shape(fields, nodes, slots),
        [SMEM] + [VMEM] * 6,
        [pltpu.VMEM((2 * LANES, slots), F32)],
    )(place, assembled, face_lists, low1, high1, near_low1, near_high1)
    return (out, grad.reshape(PARAMS))


def solution(mesh):
    return jax.shard_map(
        per_device,
        mesh=mesh,
        in_specs=(
            P("segment", None, None, None, ("region", "dom")),
            P(("region", "dom"), None),
            P(None, None, ("region", "dom")),
            P(),
            P(),
            P(None, ("region", "dom")),
            P(("region", "dom")),
        ),
        out_specs=(P(None, None, ("region", "dom")), P()),
        check_vma=False,
    )
```

```python
import functools

import jax
import jax.numpy as jnp
from jax import lax
from jax.experimental import pallas as pl
from jax.experimental.pallas import tpu as pltpu
from jax.sharding import PartitionSpec as P

FACE_NODES = 25
STEPS = 2
PARAMS = 4096
LANES = 128
RIDE = PARAMS // (4 * LANES)

rk_weights = (1.0 / 6.0, 1.0 / 3.0, 1.0 / 3.0, 1.0 / 6.0)
step_size = 0.5
face_gain = 0.5

F32 = jnp.float32
BF16 = jnp.bfloat16
VMEM = pl.BlockSpec(memory_space=pltpu.VMEM)
SMEM = pl.BlockSpec(memory_space=pltpu.SMEM)
NN = (((1,), (0,)), ((), ()))
NT = (((1,), (1,)), ((), ()))


def call(body, outs, specs, scratch=(), flops=1e6, moved=1e4):
    return pl.pallas_call(
        body,
        out_shape=outs,
        in_specs=specs,
        out_specs=jax.tree.map(lambda _: VMEM, outs),
        scratch_shapes=list(scratch),
        compiler_params=pltpu.CompilerParams(vmem_limit_bytes=40 * 2**20),
        cost_estimate=pl.CostEstimate(
            flops=int(flops), bytes_accessed=int(moved), transcendentals=0
        ),
    )


def shape(*dims, dtype=F32):
    return jax.ShapeDtypeStruct(dims, dtype)


def halves(value):
    top = value.astype(BF16)
    return top, (value - top.astype(F32)).astype(BF16)


def dot(a, b, dims=NN):
    return lax.dot_general(a, b, dims, preferred_element_type=F32)


def pick(value, chosen, dims=NN):
    top, rest = halves(value)
    return dot(top, chosen, dims) + dot(rest, chosen, dims)


def product(left, right):
    top, rest = halves(right)
    return dot(left[0], top) + (dot(left[0], rest) + dot(left[1], top))


def chosen_slots(listed, slots):
    rows = lax.broadcasted_iota(jnp.int32, (slots, listed.shape[1]), 0)
    return (rows == listed).astype(F32).astype(BF16)


def stacked(value):
    top, rest = halves(value)
    return jnp.concatenate(
        [jnp.concatenate([top, top], axis=1), jnp.concatenate([rest, rest], axis=1)], axis=0
    )


def through(double, value):
    top, rest = halves(value)
    both = dot(double, jnp.concatenate([top, rest], axis=0))
    return both[:LANES] + both[LANES:]


def segment_weight(place_ref, minor, local, k, i):
    at = lax.rem(place_ref[2] + k, minor) * local + i
    weight = jnp.float32(rk_weights[0])
    for n in range(1, len(rk_weights)):
        weight = jnp.where(at == n, jnp.float32(rk_weights[n]), weight)
    return weight


def states_kernel(local, fields, nodes, rows_ref, *outs):
    parts = rows_ref.shape[0] // (local * fields * nodes * STEPS)
    stride = parts * STEPS
    for step in range(STEPS):
        for n in range(local * fields):
            for c in range(parts):
                start = n * nodes * stride + c * STEPS + step
                outs[step][n * LANES : n * LANES + nodes, c * LANES : (c + 1) * LANES] = rows_ref[
                    pl.ds(start, nodes, stride=stride), :
                ]
            outs[step][n * LANES + nodes : (n + 1) * LANES, :] = jnp.zeros(
                (LANES - nodes, parts * LANES), F32
            )


def start_kernel(place_ref, a_ref, lists_ref, one_ref, two_ref, face_ref):
    fields, nodes, slots = a_ref.shape
    face_ref[...] = jnp.zeros_like(face_ref)
    for f in range(fields):
        face_ref[0, pl.ds(f * FACE_NODES, FACE_NODES), :] = a_ref[f, 0:FACE_NODES, :]
        face_ref[1, pl.ds(f * FACE_NODES, FACE_NODES), :] = a_ref[f, nodes - FACE_NODES : nodes, :]
    low = pick(face_ref[0], chosen_slots(lists_ref[0:1, :], slots))
    high = pick(face_ref[1], chosen_slots(lists_ref[1:2, :], slots))
    put_traces(place_ref, low, high, one_ref, two_ref)


def put_traces(place_ref, low, high, one_ref, two_ref):
    even = place_ref[4] == 0
    one_ref[0:LANES, :] = jnp.where(even, high, low)
    two_ref[0:LANES, :] = jnp.where(even, low, high)


def face_rows(place_ref, lists_ref, one_ref, two_ref, near_one_ref, near_two_ref, slots, to_ref):
    gain = step_size * face_gain
    even = place_ref[4] == 0
    one = gain * (near_one_ref[0:LANES, :] - one_ref[0:LANES, :])
    near_two = jnp.where(place_ref[5] > 0, near_two_ref[0:LANES, :], 0.0)
    two = gain * (near_two - two_ref[0:LANES, :])
    to_ref[0:LANES, :] = pick(
        jnp.where(even, two, one), chosen_slots(lists_ref[0:1, :], slots), NT
    )
    to_ref[LANES : 2 * LANES, :] = pick(
        jnp.where(even, one, two), chosen_slots(lists_ref[1:2, :], slots), NT
    )


def outgoing_kernel(
    cap, major, minor, place_ref, a_ref, map_ref, lists_ref, one_ref, two_ref, near_one_ref, near_two_ref, *refs
):
    outs, (f_ref, all_ref, turned_ref) = refs[:major], refs[major:]
    fields, nodes, slots = a_ref.shape
    wide = fields * LANES
    all_ref[0:wide, :] = jnp.zeros((wide, slots), F32)
    for f in range(fields):
        all_ref[pl.ds(f * LANES, nodes), :] = a_ref[f]
    all_ref[nodes : nodes + 1, :] = map_ref[...].astype(F32)
    face_rows(place_ref, lists_ref, one_ref, two_ref, near_one_ref, near_two_ref, slots, f_ref)
    all_ref[wide:, :] = f_ref[...]
    turned_ref[...] = all_ref[...].T
    for j in range(major):
        s = lax.rem(place_ref[0] - j + major, major) * minor + place_ref[2]
        outs[j][...] = turned_ref[pl.ds(pl.multiple_of(s * cap, 8), cap), :]


def operator_kernel(deriv_ref, mixing_ref, top_ref, rest_ref, sum_ref, pad_ref):
    directions, nodes, _ = deriv_ref.shape
    fields = top_ref.shape[0] // LANES
    pad_ref[...] = jnp.zeros_like(pad_ref)
    turned = []
    for d in range(directions):
        pad_ref[0:nodes, 0:nodes] = deriv_ref[d]
        turned.append(pad_ref[...].T)
    sum_ref[...] = functools.reduce(lambda a, b: a + b, turned)
    for f in range(fields):
        for g in range(fields):
            block = mixing_ref[g * fields + f] * turned[0]
            for d in range(1, directions):
                block = block + mixing_ref[(d * fields + g) * fields + f] * turned[d]
            top, rest = halves(block)
            top_ref[f * LANES : (f + 1) * LANES, g * LANES : (g + 1) * LANES] = top
            rest_ref[f * LANES : (f + 1) * LANES, g * LANES : (g + 1) * LANES] = rest


def linear_kernel(a_in_ref, f_ref, top_ref, rest_ref, now_ref, face_ref, x_ref):
    fields, nodes, _ = a_in_ref.shape
    x_ref[...] = jnp.zeros_like(x_ref)
    for f in range(fields):
        x_ref[pl.ds(f * LANES, nodes), :] = a_in_ref[f]
    op = (top_ref[...], rest_ref[...])
    x = x_ref[...]
    now_ref[...] = x + step_size * product(op, x)
    add_faces(now_ref, f_ref, fields, nodes)
    take_faces(now_ref, face_ref, fields, nodes)


def again_kernel(now_ref, top_ref, rest_ref, base_ref):
    now = now_ref[...]
    base_ref[...] = now + step_size * product((top_ref[...], rest_ref[...]), now)


def add_faces(to_ref, face_ref, fields, nodes):
    for f in range(fields):
        at = f * LANES
        rows = f * FACE_NODES
        to_ref[pl.ds(at, FACE_NODES), :] += face_ref[pl.ds(rows, FACE_NODES), :]
        to_ref[pl.ds(at + nodes - FACE_NODES, FACE_NODES), :] += face_ref[
            pl.ds(LANES + rows, FACE_NODES), :
        ]


def take_faces(from_ref, face_ref, fields, nodes):
    face_ref[...] = jnp.zeros_like(face_ref)
    for f in range(fields):
        at = f * LANES
        rows = f * FACE_NODES
        face_ref[pl.ds(rows, FACE_NODES), :] = from_ref[pl.ds(at, FACE_NODES), :]
        face_ref[pl.ds(LANES + rows, FACE_NODES), :] = from_ref[
            pl.ds(at + nodes - FACE_NODES, FACE_NODES), :
        ]


def ready_kernel(local, minor, place_ref, sum_ref, *refs):
    states, outs = refs[:STEPS], refs[STEPS:]
    fields = states[0].shape[0] // (local * LANES)
    double = stacked(sum_ref[...].T)
    for step in range(STEPS):
        for i in range(local):
            prepare(states[step], outs[2 * step], outs[2 * step + 1], double, segment_weight(place_ref, minor, local, 0, i), i, fields, i == 0)


def prepare(state_ref, r_ref, mean_ref, double, weight, i, fields, first):
    for f in range(fields):
        at = (i * fields + f) * LANES
        u = state_ref[at : at + LANES, :]
        part = jnp.tanh(u) * through(double, u)
        rows = slice(f * LANES, (f + 1) * LANES)
        if f == 0:
            r_ref[i * LANES : (i + 1) * LANES, :] = part
        else:
            r_ref[i * LANES : (i + 1) * LANES, :] += part
        if first:
            mean_ref[rows, :] = weight * u
        else:
            mean_ref[rows, :] += weight * u


def advance(minor, local, place_ref, states, r_ref, mean_ref, a_ref, op, sum_ref, t_ref, r_more_ref, mean_more_ref, q_ref, sums_ref):
    wide, elems = a_ref.shape
    fields = wide // LANES
    double = stacked(sum_ref[...].T)
    forward = stacked(sum_ref[...])
    linear = product(op, a_ref[...])
    dense = jnp.zeros((LANES, elems), F32)
    mean_more_ref[...] = mean_ref[...]
    for k in range(minor):
        for i in range(local):
            weight = segment_weight(place_ref, minor, local, k, i)
            if k:
                prepare(states[k], r_more_ref, mean_more_ref, double, weight, i, fields, False)
            r = (r_more_ref if k else r_ref)[i * LANES : (i + 1) * LANES, :]
            p = jnp.zeros((LANES, elems), F32)
            for f in range(fields):
                at = (i * fields + f) * LANES
                q = jnp.tanh(states[k][at : at + LANES, :])
                q_ref[f * LANES : (f + 1) * LANES, :] = q
                p = p + q * a_ref[f * LANES : (f + 1) * LANES, :]
            p = weight * p
            dense = dense + p * r
            for f in range(fields):
                rows = slice(f * LANES, (f + 1) * LANES)
                if k + i == 0:
                    sums_ref[rows, :] = q_ref[rows, :] * p
                else:
                    sums_ref[rows, :] += q_ref[rows, :] * p
    for f in range(fields):
        rows = slice(f * LANES, (f + 1) * LANES)
        dense = dense + linear[rows, :] * mean_more_ref[rows, :]
        volume = linear[rows, :] + through(forward, sums_ref[rows, :])
        t_ref[rows, :] = a_ref[rows, :] + step_size * volume
    return jnp.sum(dense, axis=0, keepdims=True)


def slots_of(owner_ref, place_ref, cap, major, minor):
    elems = owner_ref.shape[1]
    owner = owner_ref[...]
    doms = -(-major * minor // 8) * 8
    rows = lax.broadcasted_iota(jnp.int32, (doms, elems), 0)
    named = (rows == owner).astype(F32)
    before = lax.broadcasted_iota(jnp.int32, (elems, elems), 0)
    after = lax.broadcasted_iota(jnp.int32, (elems, elems), 1)
    earlier = dot(named.astype(BF16), (before < after).astype(F32).astype(BF16))
    rank = jnp.sum(named * earlier, axis=0, keepdims=True).astype(jnp.int32)
    high = jnp.zeros_like(owner)
    for k in range(1, major):
        high = high + (owner >= k * minor).astype(jnp.int32)
    low = owner - high * minor
    high = high - place_ref[0]
    low = low - place_ref[2]
    high = jnp.where(high < 0, high + major, high)
    low = jnp.where(low < 0, low + minor, low)
    slot = (high * minor + low) * cap + rank
    return jnp.where(place_ref[3] > 0, slot, -1)


def first_kernel(cap, major, minor, local, nodes, place_ref, owner_ref, top_ref, rest_ref, sum_ref, r_ref, mean_ref, *refs):
    states, refs = refs[:minor], refs[minor:]
    blocks, refs = refs[: major * minor], refs[major * minor :]
    face_outs, refs = refs[:major], refs[major:]
    now_ref, more_ref, got_ref, a_ref, fx_ref = refs[:5]
    elems = owner_ref.shape[1]
    slots = cap * major * minor
    wide = now_ref.shape[0]
    fields = wide // LANES
    slot = slots_of(owner_ref, place_ref, cap, major, minor)
    rows = lax.broadcasted_iota(jnp.int32, (slots, elems), 0)
    chosen = (rows == slot).astype(F32).astype(BF16)
    for n, block in enumerate(blocks):
        got_ref[n * cap : (n + 1) * cap, :] = block[...]
    here = pick(got_ref[...].T, chosen)
    a_ref[...] = here[0:wide]
    fx_ref[...] = here[wide:]
    param = a_ref[nodes : nodes + 1, :]
    op = (top_ref[...], rest_ref[...])
    density = advance(
        minor, local, place_ref, states, r_ref, mean_ref, a_ref, op, sum_ref, now_ref, *refs[5:]
    )
    add_faces(now_ref, fx_ref, fields, nodes)
    take_faces(now_ref, fx_ref, fields, nodes)
    fx_ref[LANES - 3 : LANES - 2, :] = jnp.ones((1, elems), F32)
    sent = pick_back(chosen, fx_ref[...])
    width = cap * minor
    for k in range(major):
        face_outs[k][...] = sent[k * width : (k + 1) * width, :]
    more_ref[...] = jnp.concatenate(
        [density, param, slot.astype(F32), jnp.zeros((5, elems), F32)], axis=0
    )


def pick_back(chosen, value):
    top, rest = halves(value)
    return dot(chosen, top, NT) + dot(chosen, rest, NT)


def second_kernel(cap, major, minor, local, nodes, place_ref, now_ref, more_ref, top_ref, rest_ref, sum_ref, r_ref, mean_ref, *refs):
    states, refs = refs[:minor], refs[minor:]
    outs, refs = refs[: major * minor], refs[major * minor :]
    t_ref = refs[0]
    wide, elems = now_ref.shape
    fields = wide // LANES
    slots = cap * major * minor
    op = (top_ref[...], rest_ref[...])
    density = advance(
        minor, local, place_ref, states, r_ref, mean_ref, now_ref, op, sum_ref, t_ref, *refs[1:]
    )
    t_ref[nodes : nodes + 1, :] = jnp.ones((1, elems), F32)
    slot = more_ref[2:3, :].astype(jnp.int32)
    rows = lax.broadcasted_iota(jnp.int32, (slots, elems), 0)
    chosen = (rows == slot).astype(F32).astype(BF16)
    sent = pick_back(chosen, t_ref[...])
    density = (more_ref[0:1, :] + density) * (1.0 / (fields * nodes))
    density = jnp.where(slot >= 0, density, 0.0)
    param = more_ref[1:2, :].astype(jnp.int32)
    count = PARAMS // LANES
    high = lax.shift_right_logical(param, 7)
    low = param - high * LANES
    in_high = lax.broadcasted_iota(jnp.int32, (count, elems), 0) == high
    in_low = (lax.broadcasted_iota(jnp.int32, (LANES, elems), 0) == low).astype(F32).astype(BF16)
    grad = pick(jnp.where(in_high, density, 0.0), in_low, NT)
    for n, out in enumerate(outs):
        out[0:cap, 0:wide] = sent[n * cap : (n + 1) * cap, :]
        out[cap : cap + RIDE, :] = jnp.zeros((RIDE, wide), F32)
        for m in range(4):
            out[cap : cap + RIDE, m * LANES : (m + 1) * LANES] = grad[m * RIDE : (m + 1) * RIDE, :]


def place_block(place_ref, got_ref, block, cap, major, minor, j, k):
    s = lax.rem(place_ref[0] - j + major, major) * minor
    s = s + lax.rem(place_ref[2] - k + minor, minor)
    got_ref[pl.ds(pl.multiple_of(s * cap, 8), cap), :] = block


def faces_kernel(cap, major, minor, place_ref, base_ref, lists_ref, *refs):
    one_ref, two_ref, got_ref = refs[minor:]
    for k in range(minor):
        for j in range(major):
            place_block(place_ref, got_ref, refs[k][j * cap : (j + 1) * cap, :], cap, major, minor, j, k)
    slots = got_ref.shape[0]
    turned = got_ref[...].T
    mine = turned[LANES - 3 : LANES - 2, :] > 0.5
    now = jnp.where(mine, turned, base_ref[...])
    low = pick(now[0:LANES], chosen_slots(lists_ref[0:1, :], slots))
    high = pick(now[LANES:], chosen_slots(lists_ref[1:2, :], slots))
    put_traces(place_ref, low, high, one_ref, two_ref)
    grad = refs[0][major * cap :, :]
    for k in range(1, minor):
        grad = grad + refs[k][major * cap :, :]
    for m in range(4):
        rows = slice(m // 2 * RIDE, (m // 2 + 1) * RIDE)
        at = LANES + m * RIDE
        part = grad[rows, m % 2 * LANES : (m % 2 + 1) * LANES]
        one_ref[at : at + RIDE, :] = part
        two_ref[at : at + RIDE, :] = part


def assemble_kernel(nodes, cap, major, minor, place_ref, base_ref, *refs):
    out_ref, got_ref = refs[minor:]
    for k in range(minor):
        for j in range(major):
            place_block(place_ref, got_ref, refs[k][j * cap : (j + 1) * cap, :], cap, major, minor, j, k)
    turned = got_ref[...].T
    mine = turned[nodes : nodes + 1, :] > 0.5
    out_ref[...] = jnp.where(mine, turned, base_ref[...])


def last_kernel(place_ref, now_ref, lists_ref, one_ref, two_ref, near_one_ref, near_two_ref, out_ref, face_ref):
    fields, nodes, slots = out_ref.shape
    face_rows(place_ref, lists_ref, one_ref, two_ref, near_one_ref, near_two_ref, slots, face_ref)
    for f in range(fields):
        out_ref[f] = now_ref[pl.ds(f * LANES, nodes), :]
        rows = f * FACE_NODES
        out_ref[f, 0:FACE_NODES, :] += face_ref[pl.ds(rows, FACE_NODES), :]
        out_ref[f, nodes - FACE_NODES : nodes, :] += face_ref[pl.ds(LANES + rows, FACE_NODES), :]


def after(value, *earlier):
    return lax.optimization_barrier((value, *earlier))[0]


def across(one, two, ends):
    size = lax.axis_size("region")
    near = []
    for value, first in ((one, 0), (two, 1)):
        pairs = [(i, i + 1) for i in range(first, size - 1, 2)]
        if ends and first and size == 4:
            pairs = pairs + [(0, 3)]
        near.append(lax.ppermute(value, "region", pairs + [(j, i) for i, j in pairs]))
    return near


def over_regions(value, near_one, near_two):
    size = lax.axis_size("region")
    if size == 4:
        far = lax.ppermute(value, "region", [(i, i ^ 2) for i in range(size)])
        return (value + near_one) + (near_two + far)
    return lax.psum(value, "region")


def per_device(stored, new_owner, adjoint, deriv, mixing, face_lists, param_map):
    minor = lax.axis_size("segment")
    dom_count = lax.axis_size("dom")
    major = dom_count // minor
    local, _, fields, nodes, elems = stored.shape
    slots = adjoint.shape[2]
    faces = face_lists.shape[1]
    cap = slots // dom_count
    wide = fields * LANES
    axes = ("dom", "segment")
    ys, xs = range(major), range(minor)

    def at(sy, c, x):
        return (sy * minor + c % minor) * minor + x % minor

    def move(value, pairs):
        return lax.ppermute(value, axes, pairs)

    def to_workers(parts):
        got = []
        for j in range(major):
            for k in range(minor):
                pairs = [(at((y + j) % major, x + k, x), at(y, x, x)) for y in ys for x in xs]
                got.append(move(parts[j], pairs) if j + k else parts[j])
        return got

    def from_workers(parts):
        got = []
        for j in range(major):
            total = None
            for k in range(minor):
                pairs = [(at(y, x, x), at((y + j) % major, x + k, x)) for y in ys for x in xs]
                part = parts[j * minor + k]
                part = move(part, pairs) if j + k else part
                total = part if total is None else total + part
            got.append(total)
        return got

    def to_segment(value, k):
        return lax.ppermute(value, "segment", [(x, (x + k) % minor) for x in xs])

    dom = lax.axis_index("dom")
    seg = lax.axis_index("segment")
    region = lax.axis_index("region")
    size = lax.axis_size("region")
    second = 1 - ((region == 0) | ((region == size - 1) & (size % 2 == 0))).astype(jnp.int32)
    ty, tc = dom // minor, dom % minor
    place = jnp.stack([ty, tc, seg, (tc == seg).astype(jnp.int32), region % 2, second]).astype(jnp.int32)
    owner = new_owner.reshape(1, elems)
    mapped = param_map.reshape(1, slots)

    rows = stored.reshape(local, STEPS, fields, nodes, elems // LANES, LANES)
    rows = rows.transpose(0, 2, 3, 4, 1, 5).reshape(-1, LANES)
    own = call(
        functools.partial(states_kernel, local, fields, nodes),
        (shape(local * wide, elems),) * STEPS,
        [VMEM],
    )(rows)
    states = [
        [own[step]]
        + [
            lax.ppermute(
                own[step], axes, [(at(y, x, x + k), at(y, x, x)) for y in ys for x in xs]
            )
            for k in range(1, minor)
        ]
        for step in range(STEPS)
    ]

    trace = shape(LANES, faces)
    low, high = call(
        start_kernel,
        (trace, trace),
        [SMEM] + [VMEM] * 2,
        [pltpu.VMEM((2, LANES, slots), F32)],
    )(place, adjoint, face_lists)
    near_low, near_high = across(low, high, False)
    top, rest, total = call(
        operator_kernel,
        (shape(wide, wide, dtype=BF16), shape(wide, wide, dtype=BF16), shape(LANES, LANES)),
        [VMEM, SMEM],
        [pltpu.VMEM((LANES, LANES), F32)],
    )(deriv, mixing.reshape(-1))
    ready = call(
        functools.partial(ready_kernel, local, minor),
        (shape(local * LANES, elems), shape(wide, elems)) * STEPS,
        [SMEM] + [VMEM] * (1 + STEPS),
    )(place, total, *own)

    sent = wide + 2 * LANES
    *a_out, f0 = call(
        functools.partial(outgoing_kernel, cap, major, minor),
        (shape(cap, sent),) * major + (shape(2 * LANES, slots),),
        [SMEM] + [VMEM] * 7,
        [pltpu.VMEM((sent, slots), F32), pltpu.VMEM((slots, sent), F32)],
    )(place, adjoint, mapped, face_lists, low, high, near_low, near_high)
    blocks = to_workers(a_out)

    base_once, base_face = call(
        linear_kernel,
        (shape(wide, slots), shape(2 * LANES, slots)),
        [VMEM] * 4,
        [pltpu.VMEM((wide, slots), F32)],
    )(adjoint, f0, top, rest)
    blocks[-1] = after(blocks[-1], base_once, base_face)

    work = [
        pltpu.VMEM((local * LANES, elems), F32),
        pltpu.VMEM((wide, elems), F32),
        pltpu.VMEM((wide, elems), F32),
        pltpu.VMEM((wide, elems), F32),
    ]
    *face_parts, now, more = call(
        functools.partial(first_kernel, cap, major, minor, local, nodes),
        (shape(cap * minor, 2 * LANES),) * major + (shape(wide, elems), shape(8, elems)),
        [SMEM] + [VMEM] * (6 + minor + dom_count),
        [
            pltpu.VMEM((slots, sent), F32),
            pltpu.VMEM((wide, elems), F32),
            pltpu.VMEM((2 * LANES, elems), F32),
        ]
        + work,
    )(place, owner, top, rest, total, *ready[0:2], *states[0], *blocks)

    moved = [face_parts[0]] + [
        move(face_parts[j], [(at(y, x, x), at((y + j) % major, x, x)) for y in ys for x in xs])
        for j in range(1, major)
    ]
    parts = call(
        functools.partial(second_kernel, cap, major, minor, local, nodes),
        (shape(cap + RIDE, wide),) * dom_count,
        [SMEM] + [VMEM] * (7 + minor),
        [pltpu.VMEM((wide, elems), F32)] + work,
        moved=4e7,
    )(place, now, more, top, rest, total, *ready[2:4], *states[1])
    moved[-1] = after(moved[-1], *parts)
    joined = [
        jnp.concatenate([part[k * cap : (k + 1) * cap] for part in moved]) for k in range(minor)
    ]
    faces_mine = joined[0]
    for k in range(1, minor):
        pairs = [(at(y, x, x), at(y, x + k, x)) for y in ys for x in xs]
        faces_mine = faces_mine + move(joined[k], pairs)
    got = from_workers(parts)
    grad = sum(value[cap:, 0 : 4 * LANES] for value in got)
    mine = jnp.concatenate([faces_mine, grad[:, 0 : 2 * LANES], grad[:, 2 * LANES :]])
    face_blocks = [mine] + [to_segment(mine, k) for k in range(1, minor)]
    mine = jnp.concatenate([value[0:cap] for value in got])
    last_blocks = [mine] + [to_segment(mine, k) for k in range(1, minor)]
    base = call(again_kernel, shape(wide, slots), [VMEM] * 3)(after(base_once, mine), top, rest)
    face_blocks[-1] = after(face_blocks[-1], mine, base)
    low1, high1 = call(
        functools.partial(faces_kernel, cap, major, minor),
        (shape(LANES + 4 * RIDE, faces),) * 2,
        [SMEM] + [VMEM] * (2 + minor),
        [pltpu.VMEM((slots, 2 * LANES), F32)],
    )(place, base_face, face_lists, *face_blocks)
    near_low1, near_high1 = across(low1, high1, True)
    grad = over_regions(low1[LANES:], near_low1[LANES:], near_high1[LANES:])

    assembled = call(
        functools.partial(assemble_kernel, nodes, cap, major, minor),
        shape(wide, slots),
        [SMEM] + [VMEM] * (1 + minor),
        [pltpu.VMEM((slots, wide), F32)],
        moved=8e7,
    )(place, base, *last_blocks)
    out = call(
        last_kernel,
        shape(fields, nodes, slots),
        [SMEM] + [VMEM] * 6,
        [pltpu.VMEM((2 * LANES, slots), F32)],
    )(place, assembled, face_lists, low1, high1, near_low1, near_high1)
    return (out, grad.reshape(PARAMS))


def solution(mesh):
    return jax.shard_map(
        per_device,
        mesh=mesh,
        in_specs=(
            P("segment", None, None, None, ("region", "dom")),
            P(("region", "dom"), None),
            P(None, None, ("region", "dom")),
            P(),
            P(),
            P(None, ("region", "dom")),
            P(("region", "dom")),
        ),
        out_specs=(P(None, None, ("region", "dom")), P()),
        check_vma=False,
    )
```
